32 devices in a mesh: region: 8 (over z, y), col: 4 (over x, core).
Axes of the slice: x: 2, y: 2, z: 4, core: 2. Of those that a mesh axis runs over, the one named last changes fastest.
Arguments:
- basis_v: bfloat16 [49152, 512], P('region', 'col'), may hold values from -6 to 6
- basis_w: bfloat16 [49152, 512], P(('region', 'col')), may hold values from -0.0546875 to 0.0546875
- couplings: bfloat16 [384, 48, 128, 128], P('region', 'col'), may hold values from -0.078125 to 0.078125
- coupling_cols: int32 [384, 48], P('region', 'col'), may hold values from 0 to 383, as said below
Outputs:
- reduced: float32 [512, 512], P(('region', 'col'))
The draws below stay inside these ranges and needn't reach their ends.
Inputs may be any that keep to these rules, and one draw needn't show every extreme that they name: `coupling_cols`: the 48 block columns of one block row are distinct and differ from its row number by at most 48; every block row takes the columns at distance 48 on both sides where they exist.
All inputs are finite; a program needn't handle non-finite values.
Results may differ from the reference program's by a relative error of at most 0.0003.
Values may be sent and summed in bfloat16 or wider, within the bound.
No kernel may reach another device: no remote copies, remote signals or barrier semaphores. Data moves between devices by JAX's collectives and lax.ppermute only.
A program may use at most 192 MiB of HBM per device.

```python
import math
import jax
import jax.numpy as jnp
from jax import lax

BLOCK = 128
BASIS = 512
SLOTS = 48
REACH = 48
BLOCK_ROWS = 384
STATES = 49152


def draw_coupling_cols(key, part):
    span = 2 * REACH + 1
    row_ids = jnp.arange(BLOCK_ROWS, dtype=jnp.int32)[:, None]
    offsets = jnp.arange(span, dtype=jnp.int32)[None, :] - REACH
    targets = row_ids + offsets
    valid = (targets >= 0) & (targets < BLOCK_ROWS)
    scores = jax.random.randint(key, (BLOCK_ROWS, span), 0, 2 ** 20, dtype=jnp.int32)
    scores = scores * span + jnp.arange(span, dtype=jnp.int32)[None, :]
    extreme = (offsets == REACH) | (offsets == -REACH)
    scores = jnp.where(extreme, scores + 2 ** 28, scores)
    scores = jnp.where(valid, scores, -1 - jnp.arange(span, dtype=jnp.int32)[None, :])
    unused, chosen = lax.top_k(scores, SLOTS)
    return jnp.take_along_axis(targets, chosen, axis=1).astype(jnp.int32)


def with_spikes(entries, rng, source, target, blocks, factor):
    owner, partner = [(jnp.arange(entries.shape[dim]) // (entries.shape[dim] // blocks)).reshape([-1 if axis == dim else 1 for axis in range(entries.ndim)]) for dim in (source, target)]
    chosen = jax.random.permutation(rng, blocks)[partner]
    strong = (owner == chosen) | (owner == (partner + blocks // 2) % blocks)
    return jnp.where(strong, factor * entries, entries)


def block_levels(stream_key, extent, split, low, largest):
    def one(axis_at, parts):
        heights = jax.random.uniform(jax.random.fold_in(jax.random.fold_in(stream_key, 6), axis_at), (parts,), jnp.float32, low / len(split), largest / len(split))
        return jnp.repeat(jnp.exp(heights), extent[axis_at] // parts).reshape((-1,) + (1,) * (len(extent) - axis_at - 1))

    gain = one(*split[0])
    for cut in split[1:]:
        gain = gain * one(*cut)
    return gain


def centred(key, extent, spread, bound, shards=(), kind=jnp.bfloat16):
    drawn = spread * jax.random.normal(key, extent, jnp.float32)
    if shards:
        drawn = drawn * block_levels(key, extent, shards, -0.22, 0.18)
    return jnp.clip(drawn, -bound, bound).astype(kind)


def gaussian_with(stream_key, dims, deviation, most, split, heavy, kind=jnp.bfloat16):
    result = deviation * jax.random.normal(stream_key, dims, jnp.float32)
    if split:
        result = result * block_levels(stream_key, dims, split, -0.22, 0.18)
    return jnp.clip(with_spikes(result, jax.random.fold_in(stream_key, 3), *heavy), -most, most).astype(kind)


def setup_inputs(seed: int = 0) -> dict:
    splits = jax.random.split(jax.random.key(seed), 5)
    basis_v = centred(splits[0], (STATES, BASIS), 1.0, 6.0, ((0, 8), (1, 4)))
    basis_w = gaussian_with(splits[1], (STATES, BASIS), STATES ** -0.5, 0.0546875, ((0, 32),), (0, 1, 32, 2.75))
    couplings = centred(splits[2], (BLOCK_ROWS, SLOTS, BLOCK, BLOCK), (SLOTS * BLOCK) ** -0.5, 0.078125, ((0, 8), (1, 4)))
    coupling_cols = draw_coupling_cols(jax.random.fold_in(splits[4], 71), 0)
    return dict(basis_v=basis_v, basis_w=basis_w, couplings=couplings, coupling_cols=coupling_cols)


def reference(basis_v, basis_w, couplings, coupling_cols):
    block_rows = coupling_cols.shape[0]
    block = couplings.shape[2]
    width = basis_v.shape[1]
    per_group = math.gcd(block_rows, 16)
    v_blocks = basis_v.reshape(block_rows, block, width)
    a_groups = couplings.reshape(block_rows // per_group, per_group, SLOTS, block, block)
    c_groups = coupling_cols.reshape(block_rows // per_group, per_group, SLOTS)
    w_groups = basis_w.reshape(block_rows // per_group, per_group * block, width)

    def advance(running, operands):
        blocks, columns, w_rows = operands
        picked = v_blocks[columns].astype(jnp.float32)
        coupled_image = jnp.einsum("gkrs,gksc->grc", blocks.astype(jnp.float32), picked, precision=lax.Precision.HIGHEST)
        coupled_image = coupled_image.reshape(per_group * block, width)
        running = running + jnp.einsum("rc,rd->cd", w_rows.astype(jnp.float32), coupled_image, precision=lax.Precision.HIGHEST)
        return running, None

    reduced, unused = lax.scan(advance, jnp.zeros((width, width), jnp.float32), (a_groups, c_groups, w_groups))
    return reduced
```

```python
import functools

import jax
import jax.numpy as jnp
from jax import lax
from jax.experimental import pallas as pl
from jax.experimental.pallas import tpu as pltpu
from jax.sharding import PartitionSpec as P

EVERY = ("region", "col")
VMEM = 60 * 2**20


def moved(array, axis, target):
    count = lax.axis_size(axis)
    pairs = [(i, target(i)) for i in range(count)]
    return lax.ppermute(array, axis, [(i, j) for i, j in pairs if 0 <= j < count])


def to_core(array):
    return moved(array, "col", lambda c: c ^ 1)


def to_side(array):
    return moved(array, "col", lambda c: c ^ 2)


def to_pair(array):
    return moved(array, "region", lambda r: r ^ 1)


def to_next(array):
    return moved(array, "region", lambda r: r + 2 if r % 2 == 0 else r - 2)


def largest_divisor(length, limit):
    return max(d for d in range(1, limit + 1) if length % d == 0)


def image_kernel(group, pieces, cols_ref, offs_ref, own_ref, other_ref, *refs):
    v_refs, (out_ref, v_all, sems) = refs[:pieces], refs[pieces:]
    step = pl.program_id(0)
    slots, block = own_ref.shape[1], own_ref.shape[2]

    @pl.when(step == 0)
    def _():
        copies = []
        for p in range(pieces):
            rows = v_refs[p].shape[0]
            start = pl.multiple_of(offs_ref[p] * block, block)
            copies.append(
                pltpu.make_async_copy(v_refs[p], v_all.at[pl.ds(start, rows)], sems.at[p])
            )
        for copy in copies:
            copy.start()
        for copy in copies:
            copy.wait()

    for g in range(group):
        row = step * group + g
        left, right = [], []
        for a_ref, base in ((own_ref, 0), (other_ref, slots)):
            for s in range(slots):
                start = pl.multiple_of(cols_ref[row, base + s] * block, block)
                left.append(a_ref[g, s])
                right.append(v_all[pl.ds(start, block), :])
        out_ref[g] = jnp.dot(
            jnp.concatenate(left, axis=1),
            jnp.concatenate(right, axis=0),
            preferred_element_type=jnp.float32,
        )


def image_of(cols, offs, own, other, v_pieces):
    rows, slots, block = own.shape[:3]
    width = v_pieces[0].shape[1]
    group = largest_divisor(rows, 8)
    a_spec = pl.BlockSpec((group, slots, block, block), lambda i, c, o: (i, 0, 0, 0))
    return pl.pallas_call(
        functools.partial(image_kernel, group, len(v_pieces)),
        out_shape=jax.ShapeDtypeStruct((rows, block, width), jnp.float32),
        grid_spec=pltpu.PrefetchScalarGridSpec(
            num_scalar_prefetch=2,
            grid=(rows // group,),
            in_specs=[a_spec, a_spec] + [pl.BlockSpec(memory_space=pl.ANY)] * len(v_pieces),
            out_specs=pl.BlockSpec((group, block, width), lambda i, c, o: (i, 0, 0)),
            scratch_shapes=[
                pltpu.VMEM((3 * rows * block, width), jnp.bfloat16),
                pltpu.SemaphoreType.DMA((len(v_pieces),)),
            ],
        ),
        compiler_params=pltpu.CompilerParams(vmem_limit_bytes=VMEM),
        cost_estimate=pl.CostEstimate(
            flops=4 * rows * slots * block * block * width,
            bytes_accessed=4 * rows * slots * block * block + 6 * rows * block * width,
            transcendentals=0,
        ),
        name="image",
    )(cols, offs, own, other, *v_pieces)


def project_kernel(me_ref, *refs):
    w_refs, (first_ref, second_ref, out_ref, w_all, total, sems) = refs[:4], refs[4:]
    step = pl.program_id(0)
    rows, block = first_ref.shape[0], first_ref.shape[1]
    copies = [
        pltpu.make_async_copy(w_refs[q], w_all.at[q], sems.at[q]) for q in range(4)
    ]

    @pl.when(step == 0)
    def _():
        for copy in copies:
            copy.start()
        total[...] = jnp.zeros_like(total)

    for q in range(4):
        @pl.when(step == q)
        def _():
            copies[q].wait()

    w_rows = w_all[step]
    for part, ref in enumerate((first_ref, second_ref)):
        flipped = jnp.concatenate([ref[i].T for i in range(rows)], axis=1)
        upper = flipped.astype(jnp.bfloat16)
        lower = (flipped - upper.astype(jnp.float32)).astype(jnp.bfloat16)
        both = jnp.concatenate([upper, lower], axis=0)
        product = jnp.dot(both, w_rows, preferred_element_type=jnp.float32)
        width = flipped.shape[0]
        total[part] += product[:width] + product[width:]

    @pl.when(step == 3)
    def _():
        width = total.shape[1]
        side = me_ref[0] // 2
        for part in range(2):
            place = jnp.where(side == 0, part, 1 - part)
            out_ref[place] = total[part].T


def projected(me, w_pieces, first, second):
    rows, block, width = first.shape
    length, basis = w_pieces[0].shape
    image_spec = pl.BlockSpec((rows // 4, block, width), lambda s, m: (m[0] ^ s, 0, 0))
    return pl.pallas_call(
        project_kernel,
        out_shape=jax.ShapeDtypeStruct((2, basis, width), jnp.float32),
        grid_spec=pltpu.PrefetchScalarGridSpec(
            num_scalar_prefetch=1,
            grid=(4,),
            in_specs=[pl.BlockSpec(memory_space=pl.ANY)] * 4 + [image_spec] * 2,
            out_specs=pl.BlockSpec((2, basis, width), lambda s, m: (0, 0, 0)),
            scratch_shapes=[
                pltpu.VMEM((4, length, basis), jnp.bfloat16),
                pltpu.VMEM((2, width, basis), jnp.float32),
                pltpu.SemaphoreType.DMA((4,)),
            ],
        ),
        compiler_params=pltpu.CompilerParams(vmem_limit_bytes=VMEM),
        cost_estimate=pl.CostEstimate(
            flops=8 * rows * block * basis * width,
            bytes_accessed=8 * length * basis + 8 * rows * block * width,
            transcendentals=0,
        ),
        name="project",
    )(me, *w_pieces, first, second)


def shards(basis_v, basis_w, couplings, coupling_cols):
    rows, slots, block = couplings.shape[:3]
    width = basis_v.shape[1]
    basis = basis_w.shape[1]
    regions, columns = lax.axis_size("region"), lax.axis_size("col")
    region, col = lax.axis_index("region"), lax.axis_index("col")
    odd = region % 2
    half = rows // 2

    here = coupling_cols - (region * rows - rows)
    cols = jnp.concatenate([here, to_core(here)], axis=1)
    other = to_core(couplings)

    def cut(array, which):
        start = jnp.where(odd == 1, 1 - which, which) * (half * block)
        return lax.dynamic_slice_in_dim(array, start, half * block, axis=0)

    v_parts = [cut(basis_v, 0), cut(basis_v, 1)]
    side_parts = [to_side(v) for v in v_parts]
    near_first = [to_pair(v) for v in v_parts]
    far_first = [to_next(v) for v in near_first]
    near_second = [to_pair(v) for v in side_parts]
    far_second = [to_next(v) for v in near_second]

    w_core = to_core(basis_w)
    w_side = to_side(basis_w)
    w_cross = to_core(w_side)

    near_base = jnp.where(odd == 1, 0, 2 * rows)
    far_base = jnp.where(odd == 1, 2 * rows, 0)
    own_at = [rows + odd * half, rows + (1 - odd) * half]
    near_at = [near_base + (1 - odd) * half, near_base + odd * half]
    far_at = [far_base + (1 - odd) * half, far_base + odd * half]
    first_offs = jnp.stack([jnp.int32(rows)] + near_at + far_at).astype(jnp.int32)
    second_offs = jnp.stack(own_at + near_at + far_at).astype(jnp.int32)

    first = image_of(cols, first_offs, couplings, other, [basis_v] + near_first + far_first)
    second = image_of(
        cols, second_offs, couplings, other, side_parts + near_second + far_second
    )
    me = jnp.reshape(col, (1,)).astype(jnp.int32)
    partial = projected(me, [basis_w, w_core, w_side, w_cross], first, second)

    devices = regions * columns
    tile = basis // devices
    sent = partial.reshape(2, devices, tile, width).transpose(1, 0, 2, 3)
    received = lax.all_to_all(sent, EVERY, 0, 0, tiled=True)
    summed = received.reshape(regions, columns // 2, 2, 2, tile, width).sum(axis=(0, 1))
    return summed.transpose(2, 1, 0, 3).reshape(tile, basis)


def solution(mesh):
    in_specs = (
        P("region", "col"),
        P(("region", "col"), None),
        P("region", "col", None, None),
        P("region", "col"),
    )
    out_specs = P(("region", "col"), None)
    return jax.shard_map(shards, mesh=mesh, in_specs=in_specs, out_specs=out_specs, check_vma=False)
```

```python
import functools

import jax
import jax.numpy as jnp
from jax import lax
from jax.experimental import pallas as pl
from jax.experimental.pallas import tpu as pltpu
from jax.sharding import PartitionSpec as P

EVERY = ("region", "col")
VMEM = 60 * 2**20
PAIR = 2
LANES = 8
DEPTH = 3
V_BITS, BLOCK_BITS = 8, 10


def moved(array, axis, target):
    count = lax.axis_size(axis)
    pairs = [(i, target(i)) for i in range(count)]
    return lax.ppermute(array, axis, [(i, j) for i, j in pairs if 0 <= j < count])


def to_core(array):
    return moved(array, "col", lambda c: c ^ 1)


def to_side(array):
    return moved(array, "col", lambda c: c ^ 2)


def to_near(array):
    return moved(array, "region", lambda r: r ^ 1)


def to_far(array):
    return moved(array, "region", lambda r: r + 1 if r % 2 else r - 1)


def onward(array):
    return moved(array, "region", lambda r: r - 2 if r % 2 else r + 2)


def after(array, *others):
    return lax.optimization_barrier((array, *others))[0]


def largest_divisor(length, limit):
    return max(d for d in range(1, limit + 1) if length % d == 0)


def anywhere(count):
    return [pl.BlockSpec(memory_space=pl.ANY)] * count


def image_kernel(group, parts, cols_ref, offs_ref, own_ref, other_ref, *refs):
    pieces = len(parts)
    v_refs, (out_ref, v_all, sems) = refs[:pieces], refs[pieces:]
    step = pl.program_id(0)
    slots, block = own_ref.shape[1], own_ref.shape[2]

    @pl.when(step == 0)
    def _():
        v_all[...] = jnp.zeros_like(v_all)
        copies = []
        for p in range(pieces):
            rows = v_refs[p].shape[0]
            start = pl.multiple_of(offs_ref[p] * block, block)
            target = v_all.at[pl.ds(start, rows), pl.ds(parts[p] * block, block)]
            copies.append(pltpu.make_async_copy(v_refs[p], target, sems.at[p]))
        for copy in copies:
            copy.start()
        for copy in copies:
            copy.wait()

    for g in range(group):
        row = step * group + g
        left, right = [], []
        for a_ref, base in ((own_ref, 0), (other_ref, slots)):
            for s in range(slots):
                start = pl.multiple_of(cols_ref[row, base + s] * block, block)
                left.append(a_ref[g, s])
                right.append(v_all[pl.ds(start, block), :])
        product = jnp.dot(
            jnp.concatenate(left, axis=1),
            jnp.concatenate(right, axis=0),
            preferred_element_type=jnp.float32,
        )
        for part in range(2):
            out_ref[part, g] = product[:, part * block : (part + 1) * block]


def image_of(cols, offs, own, other, v_pieces, parts):
    rows, slots, block = own.shape[:3]
    group = largest_divisor(rows, 8)
    a_spec = pl.BlockSpec((group, slots, block, block), lambda i, c, o: (i, 0, 0, 0))
    return pl.pallas_call(
        functools.partial(image_kernel, group, parts),
        out_shape=jax.ShapeDtypeStruct((2, rows, block, block), jnp.float32),
        grid_spec=pltpu.PrefetchScalarGridSpec(
            num_scalar_prefetch=2,
            grid=(rows // group,),
            in_specs=[a_spec, a_spec] + anywhere(len(v_pieces)),
            out_specs=pl.BlockSpec((2, group, block, block), lambda i, c, o: (0, i, 0, 0)),
            scratch_shapes=[
                pltpu.VMEM((3 * rows * block, 2 * block), jnp.bfloat16),
                pltpu.SemaphoreType.DMA((len(v_pieces),)),
            ],
        ),
        compiler_params=pltpu.CompilerParams(vmem_limit_bytes=VMEM),
        cost_estimate=pl.CostEstimate(
            flops=8 * rows * slots * block**3,
            bytes_accessed=4 * rows * slots * block * block,
            transcendentals=0,
        ),
        name="image",
    )(cols, offs, own, other, *v_pieces)


def class_list(members, places, rows, capacity):
    sources, targets, slots = members.shape
    held = members.astype(jnp.int32)
    tasks = (held.sum(axis=2) + PAIR - 1) // PAIR
    ends = jnp.cumsum(tasks, axis=1)
    rank = jnp.cumsum(held, axis=2) - held
    at = jnp.where(members, (ends - tasks)[:, :, None] * PAIR + rank, -1)
    target = jnp.arange(targets, dtype=jnp.int32)[:, None]
    block_id = (target % rows) * slots + jnp.arange(slots, dtype=jnp.int32)[None, :]
    code = ((target << (BLOCK_BITS + V_BITS)) + (block_id << V_BITS))[None] + places
    at = at.reshape(sources, 1, targets * slots)
    code = code.reshape(sources, 1, targets * slots)
    line = jnp.arange(capacity * PAIR, dtype=jnp.int32)[None, :, None]
    codes = jnp.where(at == line, code, 0).sum(axis=2)
    most = ends[:, -1].max()
    steps = (most + LANES - 1) // LANES
    return codes.reshape(-1), jnp.reshape(steps, (1,)).astype(jnp.int32)


def capacity_of(rows, slots, parts):
    tasks = (rows * slots + rows * parts * (PAIR - 1)) // PAIR
    return -(-tasks // LANES) * LANES


def add_listed(codes_ref, steps_ref, a_refs, v_all, blocks, sems, total, first_row):
    block = blocks.shape[-1]
    per_source = LANES * PAIR
    length = codes_ref.shape[0] // len(a_refs)
    steps = steps_ref[0]

    def fetch(step):
        slot = lax.rem(step, DEPTH)
        for s, a_ref in enumerate(a_refs):
            for n in range(per_source):
                code = codes_ref[s * length + step * per_source + n]
                block_id = (code >> V_BITS) & ((1 << BLOCK_BITS) - 1)
                pltpu.make_async_copy(
                    a_ref.at[block_id], blocks.at[slot, s * per_source + n], sems.at[slot]
                ).start()

    for ahead in range(DEPTH - 1):
        @pl.when(ahead < steps)
        def _():
            fetch(ahead)

    def run():
        def one(step, carry):
            slot = lax.rem(step, DEPTH)

            @pl.when(step + DEPTH - 1 < steps)
            def _():
                fetch(step + DEPTH - 1)

            pltpu.make_async_copy(blocks.at[slot], blocks.at[slot], sems.at[slot]).wait()
            products = []
            for s in range(len(a_refs)):
                for n in range(LANES):
                    left, right = [], []
                    for g in range(PAIR):
                        at = n * PAIR + g
                        code = codes_ref[s * length + step * per_source + at]
                        if g == 0:
                            row = jnp.maximum((code >> (BLOCK_BITS + V_BITS)) - first_row, 0)
                        start = pl.multiple_of((code & ((1 << V_BITS) - 1)) * block, block)
                        left.append(blocks[slot, s * per_source + at])
                        right.append(v_all[pl.ds(start, block), :])
                    product = jnp.dot(
                        jnp.concatenate(left, axis=1),
                        jnp.concatenate(right, axis=0),
                        preferred_element_type=jnp.float32,
                    )
                    products.append((row, product))
            for row, product in products:
                total[row] += product
            return carry

        lax.fori_loop(0, steps, one, 0)

    return run


def v_copies(v_refs, v_all, sems, block):
    copies, at = [], block
    for p, ref in enumerate(v_refs):
        rows = ref.shape[0]
        copies.append(pltpu.make_async_copy(ref, v_all.at[pl.ds(at, rows)], sems.at[p]))
        at += rows
    return copies


def more_kernel(pieces, codes_ref, steps_ref, own_ref, other_ref, image_ref, *refs):
    v_refs, (out_ref, v_all, blocks, a_sems, sems) = refs[:pieces], refs[pieces:]
    block = v_all.shape[1]
    copies = v_copies(v_refs, v_all, sems, block)
    copies.append(pltpu.make_async_copy(image_ref, out_ref, sems.at[pieces]))
    for copy in copies:
        copy.start()
    run = add_listed(codes_ref, steps_ref, (own_ref, other_ref), v_all, blocks, a_sems, out_ref, 0)
    v_all[pl.ds(0, block), :] = jnp.zeros((block, block), v_all.dtype)
    for copy in copies:
        copy.wait()
    run()


def list_scratch(v_pieces, block):
    v_rows = block + sum(v.shape[0] for v in v_pieces)
    return [
        pltpu.VMEM((v_rows, block), jnp.bfloat16),
        pltpu.VMEM((DEPTH, 2 * LANES * PAIR, block, block), jnp.bfloat16),
        pltpu.SemaphoreType.DMA((DEPTH,)),
    ]


def more_image(codes, steps, own, other, image, v_pieces):
    targets, block, _ = image.shape
    return pl.pallas_call(
        functools.partial(more_kernel, len(v_pieces)),
        out_shape=jax.ShapeDtypeStruct(image.shape, jnp.float32),
        grid_spec=pltpu.PrefetchScalarGridSpec(
            num_scalar_prefetch=2,
            grid=(1,),
            in_specs=anywhere(3 + len(v_pieces)),
            out_specs=pl.BlockSpec(image.shape, lambda i, c, s: (0, 0, 0)),
            scratch_shapes=list_scratch(v_pieces, block)
            + [pltpu.SemaphoreType.DMA((len(v_pieces) + 1,))],
        ),
        compiler_params=pltpu.CompilerParams(vmem_limit_bytes=VMEM),
        cost_estimate=pl.CostEstimate(
            flops=targets * 8 * block**3, bytes_accessed=2**25, transcendentals=0
        ),
        name="more_image",
    )(codes, steps, own, other, image, *v_pieces)


def split(image):
    upper = image.astype(jnp.bfloat16)
    return upper, (image - upper.astype(jnp.float32)).astype(jnp.bfloat16)


def project_kernel(pieces, codes_ref, steps_ref, me_ref, own_ref, other_ref, image_ref, *refs):
    v_refs, w_refs, refs = refs[:pieces], refs[pieces : pieces + 4], refs[pieces + 4 :]
    out_ref, v_all, blocks, a_sems, fresh, image, w_all, sems = refs
    block = v_all.shape[1]
    copies = v_copies(v_refs, v_all, sems, block)
    for copy in copies:
        copy.start()
    run = add_listed(codes_ref, steps_ref, (own_ref, other_ref), v_all, blocks, a_sems, fresh, 0)
    later = [
        pltpu.make_async_copy(w_refs[q], w_all.at[q], sems.at[pieces + q]) for q in range(4)
    ]
    later.append(pltpu.make_async_copy(image_ref, image, sems.at[pieces + 4]))
    for copy in later:
        copy.start()
    v_all[pl.ds(0, block), :] = jnp.zeros((block, block), v_all.dtype)
    fresh[...] = jnp.zeros_like(fresh)
    for copy in copies:
        copy.wait()
    run()
    for copy in later:
        copy.wait()
    rows = fresh.shape[0]
    length = rows // 4
    out_ref[...] = jnp.zeros_like(out_ref)
    for q in range(4):
        first = (me_ref[0] ^ q) * length
        parts = [
            image[pl.ds(first, length)],
            image[pl.ds(rows + first, length)] + fresh[pl.ds(first, length)],
        ]
        here = jnp.concatenate([p.reshape(length * block, block) for p in parts], axis=1)
        for term in split(here):
            out_ref[...] += jnp.dot(w_all[q], term, preferred_element_type=jnp.float32)


def projected(codes, steps, me, own, other, image, v_pieces, w_pieces):
    targets, block, _ = image.shape
    basis, length = w_pieces[0].shape
    return pl.pallas_call(
        functools.partial(project_kernel, len(v_pieces)),
        out_shape=jax.ShapeDtypeStruct((basis, 2 * block), jnp.float32),
        grid_spec=pltpu.PrefetchScalarGridSpec(
            num_scalar_prefetch=3,
            grid=(1,),
            in_specs=anywhere(7 + len(v_pieces)),
            out_specs=pl.BlockSpec((basis, 2 * block), lambda i, c, s, m: (0, 0)),
            scratch_shapes=list_scratch(v_pieces, block)
            + [
                pltpu.VMEM((targets // 2, block, block), jnp.float32),
                pltpu.VMEM(image.shape, jnp.float32),
                pltpu.VMEM((4, basis, length), jnp.bfloat16),
                pltpu.SemaphoreType.DMA((len(v_pieces) + 5,)),
            ],
        ),
        compiler_params=pltpu.CompilerParams(vmem_limit_bytes=VMEM),
        cost_estimate=pl.CostEstimate(
            flops=4 * targets * basis * block**2, bytes_accessed=2**25, transcendentals=0
        ),
        name="projected",
    )(codes, steps, me, own, other, image, *v_pieces, *w_pieces)


def last_kernel(pieces, codes_ref, steps_ref, me_ref, own_ref, other_ref, before_ref, *refs):
    v_refs, w_refs, refs = refs[:pieces], refs[pieces : pieces + 4], refs[pieces + 4 :]
    out_ref, v_all, blocks, a_sems, fresh, w_all, sems = refs
    block = v_all.shape[1]
    rows = fresh.shape[0]
    col, side = me_ref[0], me_ref[1]
    copies = v_copies(v_refs, v_all, sems, block)
    for copy in copies:
        copy.start()
    run = add_listed(
        codes_ref, steps_ref, (own_ref, other_ref), v_all, blocks, a_sems, fresh, side * rows
    )
    later = [
        pltpu.make_async_copy(w_refs[q], w_all.at[(col ^ q) & 1], sems.at[pieces + (q & 1)])
        for q in range(4)
    ]
    for q in range(4):
        pl.when((col ^ q) >> 1 == side)(later[q].start)
    v_all[pl.ds(0, block), :] = jnp.zeros((block, block), v_all.dtype)
    fresh[...] = jnp.zeros_like(fresh)
    for copy in copies:
        copy.wait()
    run()
    for q in range(4):
        pl.when((col ^ q) >> 1 == side)(later[q].wait)
    tiles, _, tile, _ = out_ref.shape
    basis, length = w_all.shape[1:]
    total = before_ref[:, block:]
    for q in range(2):
        here = fresh[q * (rows // 2) : (q + 1) * (rows // 2)].reshape(length, block)
        for term in split(here):
            total += jnp.dot(w_all[q], term, preferred_element_type=jnp.float32)
    mine = col >> 1
    out_ref[:, mine] = before_ref[:, :block].reshape(tiles, tile, block)
    out_ref[:, 1 - mine] = total.reshape(tiles, tile, block)


def finished(codes, steps, me, own, other, before, v_pieces, w_pieces, devices):
    block = own.shape[-1]
    basis, length = w_pieces[0].shape
    shape = (devices, 2, basis // devices, block)
    whole = pl.BlockSpec(before.shape, lambda i, c, s, m: (0, 0))
    return pl.pallas_call(
        functools.partial(last_kernel, len(v_pieces)),
        out_shape=jax.ShapeDtypeStruct(shape, jnp.float32),
        grid_spec=pltpu.PrefetchScalarGridSpec(
            num_scalar_prefetch=3,
            grid=(1,),
            in_specs=anywhere(2) + [whole] + anywhere(4 + len(v_pieces)),
            out_specs=pl.BlockSpec(shape, lambda i, c, s, m: (0, 0, 0, 0)),
            scratch_shapes=list_scratch(v_pieces, block)
            + [
                pltpu.VMEM((2 * length // block, block, block), jnp.float32),
                pltpu.VMEM((2, basis, length), jnp.bfloat16),
                pltpu.SemaphoreType.DMA((len(v_pieces) + 2,)),
            ],
        ),
        compiler_params=pltpu.CompilerParams(vmem_limit_bytes=VMEM),
        cost_estimate=pl.CostEstimate(
            flops=8 * basis * length * block, bytes_accessed=2**23, transcendentals=0
        ),
        name="finished",
    )(codes, steps, me, own, other, before, *v_pieces, *w_pieces)


def shards(basis_v, basis_w, couplings, coupling_cols):
    rows, slots, block = couplings.shape[:3]
    regions, columns = lax.axis_size("region"), lax.axis_size("col")
    region, col = lax.axis_index("region"), lax.axis_index("col")
    odd = region % 2
    half = rows // 2
    quarter = half // 2

    def cut(array, which):
        start = jnp.where(odd == 1, 1 - which, which) * (half * block)
        return lax.dynamic_slice_in_dim(array, start, half * block, axis=0)

    here = coupling_cols - (region * rows - rows)
    there = to_core(here)
    own_a, own_b = cut(basis_v, 0), cut(basis_v, 1)
    side_a = to_side(own_a)
    near_a = to_near(own_a)
    side_b = to_side(own_b)
    near_b = to_near(own_b)
    other = to_core(after(couplings, there))
    far_a = onward(near_a)
    near_side_a = to_near(side_a)
    far_b = onward(near_b)
    near_side_b = to_near(side_b)
    w_own = basis_w.T
    w_core = to_core(after(w_own, other))
    w_side = to_side(after(w_own, side_b))
    far_side_a = onward(near_side_a)
    w_cross = to_core(w_side)
    far_side_b = [
        onward(near_side_b[: quarter * block]),
        to_far(after(side_b, near_side_a)[quarter * block :]),
    ]
    w_pieces = [w_own, w_core, w_side, w_cross]

    cols = jnp.concatenate([here, there], axis=1)
    near_base = jnp.where(odd == 1, 0, 2 * rows)
    far_base = 2 * rows - near_base
    near_at = [near_base + (1 - odd) * half, near_base + odd * half]
    own_at = [rows + odd * half, rows + (1 - odd) * half]
    offs = jnp.stack([jnp.int32(rows)] + near_at + own_at).astype(jnp.int32)

    both = jnp.stack([here, there])
    in_near = both // rows == near_base // rows
    in_far = both // rows == far_base // rows
    upper = both % rows >= half
    is_a = upper == (odd == 0)
    within = both % half
    late = jnp.where(is_a, within, half + within)
    second = class_list(
        jnp.concatenate([in_far, in_near & is_a], axis=1),
        jnp.concatenate([1 + late, 1 + rows + within], axis=1),
        rows,
        capacity_of(rows, slots, 2),
    )
    third = class_list(
        (in_near & ~is_a) | (in_far & is_a),
        jnp.where(in_near, 1 + within, 1 + half + within),
        rows,
        capacity_of(rows, slots, 1),
    )
    fourth = class_list(in_far & ~is_a, 1 + within, rows, capacity_of(rows, slots, 1))

    image = image_of(
        cols, offs, couplings, other, [basis_v, near_a, near_b, side_a, side_b], (0, 0, 0, 1, 1)
    )
    image = image.reshape(2 * rows, block, block)
    own_list = couplings.reshape(rows * slots, block, block)
    other_list = other.reshape(rows * slots, block, block)
    image = more_image(*second, own_list, other_list, image, [far_a, far_b, near_side_a])
    me = jnp.stack([col, odd]).astype(jnp.int32)
    before = projected(
        *third, me, own_list, other_list, image, [near_side_b, far_side_a], w_pieces
    )
    devices = regions * columns
    sent = finished(
        *fourth, me, own_list, other_list, before, far_side_b, w_pieces, devices
    )
    received = lax.all_to_all(sent, EVERY, 0, 0, tiled=True)
    tile = sent.shape[2]
    summed = received.reshape(regions, columns // 2, 2, 2, tile, block).sum(axis=(0, 1))
    return summed.transpose(2, 1, 0, 3).reshape(tile, columns * block)


def solution(mesh):
    in_specs = (
        P("region", "col"),
        P(("region", "col"), None),
        P("region", "col", None, None),
        P("region", "col"),
    )
    out_specs = P(("region", "col"), None)
    return jax.shard_map(shards, mesh=mesh, in_specs=in_specs, out_specs=out_specs, check_vma=False)
```

```python
import functools

import jax
import jax.numpy as jnp
from jax import lax
from jax.experimental import pallas as pl
from jax.experimental.pallas import tpu as pltpu
from jax.sharding import PartitionSpec as P

EVERY = ("region", "col")
VMEM = 60 * 2**20
PAIR = 2
LANES = 8
DEPTH = 3
V_BITS, BLOCK_BITS = 8, 10
SMALL = pl.CostEstimate(flops=1, bytes_accessed=1, transcendentals=0)
LARGE = pl.CostEstimate(flops=10**12, bytes_accessed=10**9, transcendentals=0)


def moved(array, axis, target):
    count = lax.axis_size(axis)
    pairs = [(i, target(i)) for i in range(count)]
    return lax.ppermute(array, axis, [(i, j) for i, j in pairs if 0 <= j < count])


def to_core(array):
    return moved(array, "col", lambda c: c ^ 1)


def to_side(array):
    return moved(array, "col", lambda c: c ^ 2)


def to_near(array):
    return moved(array, "region", lambda r: r ^ 1)


def to_far(array):
    return moved(array, "region", lambda r: r + 1 if r % 2 else r - 1)


def onward(array):
    return moved(array, "region", lambda r: r - 2 if r % 2 else r + 2)


def together(*arrays):
    return lax.optimization_barrier(arrays)


def after(array, *others):
    return together(array, *others)[0]


def largest_divisor(length, limit):
    return max(d for d in range(1, limit + 1) if length % d == 0)


def anywhere(count):
    return [pl.BlockSpec(memory_space=pl.ANY)] * count


def image_kernel(group, parts, fills, cols_ref, offs_ref, own_ref, other_ref, *refs):
    pieces = len(parts)
    v_refs, refs = refs[:pieces], refs[pieces:]
    out_ref, v_all, blocks, sums, v_sems, a_sems, out_sems = refs
    depth, _, _, slots, block, _ = blocks.shape
    count = out_ref.shape[1]
    groups = count // group
    first = offs_ref[pieces + len(fills)]

    def place(n, rows, part):
        start = pl.multiple_of(offs_ref[n] * block, block)
        return pl.ds(start, rows), pl.ds(part * block, block)

    def read(g):
        slot = lax.rem(g, depth)
        here = pl.ds(first + g * group, group)
        return [
            pltpu.make_async_copy(ref.at[here], blocks.at[slot, n], a_sems.at[slot, n])
            for n, ref in enumerate((own_ref, other_ref))
        ]

    def write(g):
        slot = lax.rem(g, 2)
        return pltpu.make_async_copy(
            sums.at[slot], out_ref.at[:, pl.ds(g * group, group)], out_sems.at[slot]
        )

    copies = []
    for p, ref in enumerate(v_refs):
        rows = ref.shape[0]
        target = v_all.at[place(p, rows, parts[p])]
        copies.append(pltpu.make_async_copy(ref, target, v_sems.at[p]))
    for copy in copies:
        copy.start()
    for g in range(depth - 1):
        for copy in read(g):
            copy.start()
    for n, (rows, part) in enumerate(fills):
        at = place(pieces + n, rows, part)
        v_all[at] = jnp.zeros((rows, block), v_all.dtype)
    for copy in copies:
        copy.wait()

    def one(g, carry):
        slot, out_slot = lax.rem(g, depth), lax.rem(g, 2)

        @pl.when(g + depth - 1 < groups)
        def _():
            for copy in read(g + depth - 1):
                copy.start()

        for copy in read(g):
            copy.wait()

        @pl.when(g >= 2)
        def _():
            write(g - 2).wait()

        for r in range(group):
            left, right = [], []
            for n in range(2):
                for s in range(slots):
                    code = cols_ref[first + g * group + r, n * slots + s]
                    left.append(blocks[slot, n, r, s])
                    right.append(v_all[pl.ds(pl.multiple_of(code * block, block), block), :])
            product = jnp.dot(
                jnp.concatenate(left, axis=1),
                jnp.concatenate(right, axis=0),
                preferred_element_type=jnp.float32,
            )
            for part in range(2):
                sums[out_slot, part, r] = product[:, part * block : (part + 1) * block]
        write(g).start()
        return carry

    lax.fori_loop(0, groups, one, 0)
    for g in range(max(groups - 2, 0), groups):
        write(g).wait()


def image_of(cols, own, other, v_pieces, places, parts, fills, start, count):
    rows, slots, block = own.shape[:3]
    group = largest_divisor(count, 4)
    depth = min(3, count // group + 1)
    pieces = len(v_pieces)
    offs = jnp.stack([*places, *[f[0] for f in fills], start]).astype(jnp.int32)
    fill_shapes = tuple((f[1] * block, f[2]) for f in fills)
    return pl.pallas_call(
        functools.partial(image_kernel, group, parts, fill_shapes),
        out_shape=jax.ShapeDtypeStruct((2, count, block, block), jnp.float32),
        grid_spec=pltpu.PrefetchScalarGridSpec(
            num_scalar_prefetch=2,
            grid=(1,),
            in_specs=anywhere(2 + pieces),
            out_specs=pl.BlockSpec(memory_space=pl.ANY),
            scratch_shapes=[
                pltpu.VMEM((3 * rows * block, 2 * block), jnp.bfloat16),
                pltpu.VMEM((depth, 2, group, slots, block, block), jnp.bfloat16),
                pltpu.VMEM((2, 2, group, block, block), jnp.float32),
                pltpu.SemaphoreType.DMA((pieces,)),
                pltpu.SemaphoreType.DMA((depth, 2)),
                pltpu.SemaphoreType.DMA((2,)),
            ],
        ),
        compiler_params=pltpu.CompilerParams(vmem_limit_bytes=VMEM),
        cost_estimate=SMALL,
        name="image",
    )(cols, offs, own, other, *v_pieces)


def cut_kernel(start_ref, v_ref, out_ref, stage, sems):
    start = pl.multiple_of(start_ref[0] * 128, 128)
    read = pltpu.make_async_copy(v_ref.at[pl.ds(start, stage.shape[0])], stage, sems.at[0])
    write = pltpu.make_async_copy(stage, out_ref, sems.at[1])
    read.start()
    read.wait()
    write.start()
    write.wait()


def cut(array, start, length):
    part = jax.ShapeDtypeStruct((length, array.shape[1]), array.dtype)
    return pl.pallas_call(
        cut_kernel,
        out_shape=part,
        grid_spec=pltpu.PrefetchScalarGridSpec(
            num_scalar_prefetch=1,
            grid=(1,),
            in_specs=anywhere(1),
            out_specs=pl.BlockSpec(memory_space=pl.ANY),
            scratch_shapes=[pltpu.VMEM(part.shape, part.dtype), pltpu.SemaphoreType.DMA((2,))],
        ),
        cost_estimate=SMALL,
        name="cut",
    )(jnp.reshape(start, (1,)).astype(jnp.int32), array)


def lists_kernel(rows, slots, plan, codes_ref, *refs):
    outs, steps_ref = refs[:-1], refs[-1]
    per_source = LANES * PAIR
    size = 2 * rows * slots
    lengths = [out.shape[0] // 2 for out in outs]
    turns = max(len(classes) for classes in plan)

    def one_row(row, ends):
        ends = list(ends)
        for turn in range(turns):
            active = [
                (2 * k + source, out, classes[turn] * size + (source * rows + row) * slots)
                for k, (out, classes) in enumerate(zip(outs, plan))
                if turn < len(classes)
                for source in range(2)
            ]
            for s in range(slots):
                for n, out, base in active:
                    code = codes_ref[base + s]
                    out[ends[n]] = code
                    ends[n] = ends[n] + jnp.minimum(code, 1)
            for n, out, _ in active:
                out[ends[n]] = 0
                ends[n] = ends[n] + (ends[n] & (PAIR - 1))
        return tuple(ends)

    first = tuple(jnp.int32(source * length) for length in lengths for source in range(2))
    ends = lax.fori_loop(0, rows, one_row, first)
    for k, out in enumerate(outs):
        pair = ends[2 * k], ends[2 * k + 1]
        most = jnp.maximum(pair[0], pair[1] - lengths[k])
        steps = lax.div(most + per_source - 1, per_source)
        steps_ref[k] = steps
        for source in range(2):
            def clear(at, carry, out=out):
                out[at] = 0
                return carry

            lax.fori_loop(pair[source], source * lengths[k] + steps * per_source, clear, 0)


def lists_of(codes, rows, slots, plan):
    lengths = [2 * capacity_of(rows, slots, len(c)) * PAIR for c in plan]
    smem = pl.BlockSpec(memory_space=pltpu.SMEM)
    *lists, steps = pl.pallas_call(
        functools.partial(lists_kernel, rows, slots, plan),
        out_shape=[jax.ShapeDtypeStruct((n,), jnp.int32) for n in lengths + [len(plan)]],
        in_specs=[smem],
        out_specs=[smem] * (len(plan) + 1),
        cost_estimate=SMALL,
        name="lists",
    )(codes)
    return lists, steps


def capacity_of(rows, slots, parts):
    tasks = (rows * slots + rows * parts * (PAIR - 1)) // PAIR
    return (-(-tasks // LANES) + 1) * LANES


def add_listed(codes_ref, steps, a_refs, v_all, blocks, sems, total):
    block = blocks.shape[-1]
    per_source = LANES * PAIR
    length = codes_ref.shape[0] // len(a_refs)

    def fetch(step):
        slot = lax.rem(step, DEPTH)
        for s, a_ref in enumerate(a_refs):
            for n in range(per_source):
                code = codes_ref[s * length + step * per_source + n]
                block_id = (code >> V_BITS) & ((1 << BLOCK_BITS) - 1)
                pltpu.make_async_copy(
                    a_ref.at[block_id], blocks.at[slot, s * per_source + n], sems.at[slot]
                ).start()

    for ahead in range(DEPTH - 1):
        @pl.when(ahead < steps)
        def _():
            fetch(ahead)

    def run():
        def one(step, carry):
            slot = lax.rem(step, DEPTH)

            @pl.when(step + DEPTH - 1 < steps)
            def _():
                fetch(step + DEPTH - 1)

            pltpu.make_async_copy(blocks.at[slot], blocks.at[slot], sems.at[slot]).wait()
            products = []
            for s in range(len(a_refs)):
                for n in range(LANES):
                    left, right = [], []
                    for g in range(PAIR):
                        at = n * PAIR + g
                        code = codes_ref[s * length + step * per_source + at]
                        if g == 0:
                            row = code >> (BLOCK_BITS + V_BITS)
                        start = pl.multiple_of((code & ((1 << V_BITS) - 1)) * block, block)
                        left.append(blocks[slot, s * per_source + at])
                        right.append(v_all[pl.ds(start, block), :])
                    product = jnp.dot(
                        jnp.concatenate(left, axis=1),
                        jnp.concatenate(right, axis=0),
                        preferred_element_type=jnp.float32,
                    )
                    products.append((row, product))
            for row, product in products:
                total[row] += product
            return carry

        lax.fori_loop(0, steps, one, 0)

    return run


def list_scratch(v_pieces, block):
    v_rows = block + sum(v.shape[0] for v in v_pieces)
    return [
        pltpu.VMEM((v_rows, block), jnp.bfloat16),
        pltpu.VMEM((DEPTH, 2 * LANES * PAIR, block, block), jnp.bfloat16),
        pltpu.SemaphoreType.DMA((DEPTH,)),
    ]


def copies_of(pairs, sems):
    copies = [pltpu.make_async_copy(a, b, sems.at[n]) for n, (a, b) in enumerate(pairs)]
    for copy in copies:
        copy.start()
    return copies


def v_places(v_refs, v_all, block):
    places, at = [], block
    for ref in v_refs:
        places.append((ref, v_all.at[pl.ds(at, ref.shape[0])]))
        at += ref.shape[0]
    return places


def later_kernel(pieces, codes_ref, steps_ref, me_ref, own_ref, other_ref, *refs):
    images, v_refs, refs = refs[:2], refs[2 : 2 + pieces], refs[2 + pieces :]
    out_ref, v_all, blocks, a_sems, sems = refs
    block = out_ref.shape[1]
    pairs = v_places(v_refs, v_all, block)
    for n, ref in enumerate(images):
        pairs.append((ref.at[1], out_ref.at[pl.ds(me_ref[1 + n], ref.shape[1])]))
    copies = copies_of(pairs, sems)
    run = add_listed(
        codes_ref, steps_ref[0], (own_ref, other_ref), v_all, blocks, a_sems, out_ref
    )
    v_all[pl.ds(0, block), :] = jnp.zeros((block, block), v_all.dtype)
    for copy in copies:
        copy.wait()
    run()


def later_image(codes, steps, me, own, other, images, v_pieces):
    block = own.shape[-1]
    shape = (sum(image.shape[1] for image in images), block, block)
    return pl.pallas_call(
        functools.partial(later_kernel, len(v_pieces)),
        out_shape=jax.ShapeDtypeStruct(shape, jnp.float32),
        grid_spec=pltpu.PrefetchScalarGridSpec(
            num_scalar_prefetch=3,
            grid=(1,),
            in_specs=anywhere(4 + len(v_pieces)),
            out_specs=pl.BlockSpec(shape, lambda i, *_: (0, 0, 0)),
            scratch_shapes=list_scratch(v_pieces, block)
            + [pltpu.SemaphoreType.DMA((len(v_pieces) + 2,))],
        ),
        compiler_params=pltpu.CompilerParams(vmem_limit_bytes=VMEM),
        cost_estimate=LARGE,
        name="later",
    )(codes, steps, me, own, other, *images, *v_pieces)


def last_kernel(pieces, codes_ref, steps_ref, me_ref, own_ref, other_ref, *refs):
    images, late_ref, refs = refs[:2], refs[2], refs[3:]
    v_refs, w_refs = refs[:pieces], refs[pieces : 4 + pieces]
    out_ref, v_all, blocks, a_sems, image, w_all, sems = refs[4 + pieces :]
    _, rows, block, _ = image.shape
    early = copies_of(v_places(v_refs, v_all, block) + [(late_ref, image.at[1])], sems)
    run = add_listed(
        codes_ref, steps_ref[1], (own_ref, other_ref), v_all, blocks, a_sems, image.at[1]
    )
    w_places = [(w_refs[q], w_all.at[q]) for q in range(4)]
    for n, ref in enumerate(images):
        w_places.append((ref.at[0], image.at[0, pl.ds(me_ref[1 + n], ref.shape[1])]))
    later = copies_of(w_places, sems.at[pl.ds(pieces + 1, 6)])
    v_all[pl.ds(0, block), :] = jnp.zeros((block, block), v_all.dtype)
    for copy in early:
        copy.wait()
    run()
    for copy in later:
        copy.wait()
    length = rows // 4
    total = None
    for q in range(4):
        terms = []
        for part in range(2):
            here = image[part, pl.ds((me_ref[0] ^ q) * length, length)]
            here = here.reshape(length * block, block)
            upper = here.astype(jnp.bfloat16)
            terms += [upper, (here - upper.astype(jnp.float32)).astype(jnp.bfloat16)]
        term = jnp.dot(
            w_all[q], jnp.concatenate(terms, axis=1), preferred_element_type=jnp.float32
        )
        total = term if total is None else total + term
    mine = me_ref[0] >> 1
    count, _, tile, _ = out_ref.shape
    for part, place in ((0, mine), (1, 1 - mine)):
        first = 2 * part * block
        both = total[:, first : first + block] + total[:, first + block : first + 2 * block]
        out_ref[:, place] = both.reshape(count, tile, block)


def last_projected(codes, steps, me, own, other, images, late, v_pieces, w_pieces, devices):
    rows, block, _ = late.shape
    basis, length = w_pieces[0].shape
    shape = (devices, 2, basis // devices, block)
    return pl.pallas_call(
        functools.partial(last_kernel, len(v_pieces)),
        out_shape=jax.ShapeDtypeStruct(shape, jnp.float32),
        grid_spec=pltpu.PrefetchScalarGridSpec(
            num_scalar_prefetch=3,
            grid=(1,),
            in_specs=anywhere(9 + len(v_pieces)),
            out_specs=pl.BlockSpec(shape, lambda i, *_: (0, 0, 0, 0)),
            scratch_shapes=list_scratch(v_pieces, block)
            + [
                pltpu.VMEM((2, rows, block, block), jnp.float32),
                pltpu.VMEM((4, basis, length), jnp.bfloat16),
                pltpu.SemaphoreType.DMA((len(v_pieces) + 7,)),
            ],
        ),
        compiler_params=pltpu.CompilerParams(vmem_limit_bytes=VMEM),
        cost_estimate=SMALL,
        name="last_projected",
    )(codes, steps, me, own, other, *images, late, *v_pieces, *w_pieces)


def shards(basis_v, basis_w, couplings, coupling_cols):
    rows, slots, block = couplings.shape[:3]
    regions, columns = lax.axis_size("region"), lax.axis_size("col")
    region, col = lax.axis_index("region"), lax.axis_index("col")
    odd = region % 2
    half = rows // 2

    own_a = cut(basis_v, odd * half, half * block)
    near_a, side_a = to_near(own_a), to_side(own_a)
    here = after(coupling_cols, own_a) - (region * rows - rows)
    there = to_core(here)
    w_own = basis_w.T
    w_core = to_core(after(w_own, there))
    other = to_core(after(couplings, w_core))
    own_b = cut(after(basis_v, w_core), (1 - odd) * half, half * block)
    near_b, side_b = to_near(own_b), to_side(own_b)

    cols = jnp.concatenate([here, there], axis=1)
    near_base = jnp.where(odd == 1, 0, 2 * rows)
    far_base = 2 * rows - near_base
    first, second = (1 - odd) * half, odd * half
    near_at = [near_base + first, near_base + second]
    far_at = [far_base + first, far_base + second]
    own_at = [rows + second, rows + first]
    me = jnp.stack([col, first, second]).astype(jnp.int32)

    both = jnp.stack([here, there])[None]
    in_near = both // rows == near_base // rows
    in_far = both // rows == far_base // rows
    is_a = (both % rows >= half) == (odd == 0)
    kind = jnp.arange(2, dtype=jnp.int32)[:, None, None, None]
    row = jnp.arange(rows, dtype=jnp.int32)[:, None]
    summed_early = (row >= half) == (odd == 0)
    taken = jnp.where(
        kind == 0, (in_near & (~is_a | summed_early)) | (in_far & is_a), in_far & ~is_a
    )
    piece = jnp.where(kind == 0, jnp.where(in_far, 2, jnp.where(is_a, 0, 1)), 0)
    block_id = row * slots + jnp.arange(slots, dtype=jnp.int32)[None, :]
    codes = (row << (BLOCK_BITS + V_BITS)) + (block_id << V_BITS)
    codes = jnp.where(taken, codes + 1 + piece * half + both % half, 0).reshape(-1)
    (later, last), steps = lists_of(codes, rows, slots, ((0,), (1,)))

    near_a, side_a, steps, cols, me, w_own = together(near_a, side_a, steps, cols, me, w_own)
    far_a, near_side_a = onward(near_a), to_near(side_a)

    near_b, side_b, other = together(near_b, side_b, other)
    far_b, near_side_b = onward(after(near_b, far_a)), to_near(side_b)
    w_side = to_side(after(w_own, near_b))
    pieces = [basis_v, near_a, near_b, far_a, side_a, side_b]
    at = [jnp.int32(rows), *near_at, far_at[0], *own_at]
    fills = [(far_at[1], half, 0), (near_base, rows, 1), (far_base, rows, 1)]
    early = image_of(
        cols, couplings, other, pieces, at, (0, 0, 0, 0, 1, 1), fills, first, half
    )

    early, near_side_a = together(early, near_side_a)
    far_side_a = onward(near_side_a)
    pieces = [basis_v, near_a, near_b, far_a, far_b, side_a, side_b, near_side_a]
    at = [jnp.int32(rows), *near_at, *far_at, *own_at, near_at[0]]
    fills = [(near_at[1], half, 1), (far_base, rows, 1)]
    rest = image_of(
        cols, couplings, other, pieces, at, (0, 0, 0, 0, 0, 1, 1, 1), fills, second, half
    )
    images = [early, rest]
    rest, side_b, w_side = together(rest, side_b, w_side)
    far_side_b = to_far(side_b)
    w_pieces = [w_own, w_core, w_side, to_core(w_side)]
    images = [early, rest]
    own_list = couplings.reshape(rows * slots, block, block)
    other_list = other.reshape(rows * slots, block, block)
    pieces = [near_side_a, near_side_b, far_side_a]
    image = later_image(later, steps, me, own_list, other_list, images, pieces)

    sent = last_projected(
        last, steps, me, own_list, other_list, images, image, [far_side_b], w_pieces,
        regions * columns,
    )
    received = lax.all_to_all(sent, EVERY, 0, 0, tiled=True)
    tile = sent.shape[2]
    summed = received.reshape(regions, columns // 2, 2, 2, tile, block).sum(axis=(0, 1))
    return summed.transpose(2, 1, 0, 3).reshape(tile, columns * block)


def solution(mesh):
    in_specs = (
        P("region", "col"),
        P(("region", "col"), None),
        P("region", "col", None, None),
        P("region", "col"),
    )
    out_specs = P(("region", "col"), None)
    return jax.shard_map(shards, mesh=mesh, in_specs=in_specs, out_specs=out_specs, check_vma=False)
```

```python
import functools

import jax
import jax.numpy as jnp
from jax import lax
from jax.experimental import pallas as pl
from jax.experimental.pallas import tpu as pltpu
from jax.sharding import PartitionSpec as P

EVERY = ("region", "col")
VMEM = 60 * 2**20
PAIR = 2
LANES = 8
DEPTH = 5
V_BITS, BLOCK_BITS = 8, 10
SMALL = pl.CostEstimate(flops=1, bytes_accessed=1, transcendentals=0)
LARGE = pl.CostEstimate(flops=10**12, bytes_accessed=10**9, transcendentals=0)


def moved(array, axis, target):
    count = lax.axis_size(axis)
    pairs = [(i, target(i)) for i in range(count)]
    return lax.ppermute(array, axis, [(i, j) for i, j in pairs if 0 <= j < count])


def to_core(array):
    return moved(array, "col", lambda c: c ^ 1)


def to_side(array):
    return moved(array, "col", lambda c: c ^ 2)


def to_near(array):
    return moved(array, "region", lambda r: r ^ 1)


def to_far(array):
    return moved(array, "region", lambda r: r + 1 if r % 2 else r - 1)


def onward(array):
    return moved(array, "region", lambda r: r - 2 if r % 2 else r + 2)


def together(*arrays):
    return lax.optimization_barrier(arrays)


def after(array, *others):
    return together(array, *others)[0]


def largest_divisor(length, limit):
    return max(d for d in range(1, limit + 1) if length % d == 0)


def anywhere(count):
    return [pl.BlockSpec(memory_space=pl.ANY)] * count


def image_kernel(group, parts, fills, cols_ref, offs_ref, own_ref, other_ref, *refs):
    pieces = len(parts)
    v_refs, refs = refs[:pieces], refs[pieces:]
    out_ref, v_all, blocks, sums, v_sems, a_sems, out_sems = refs
    depth, _, _, slots, block, _ = blocks.shape
    count = out_ref.shape[1]
    groups = count // group
    first = offs_ref[pieces + len(fills)]

    def place(n, rows, part):
        start = pl.multiple_of(offs_ref[n] * block, block)
        return pl.ds(start, rows), pl.ds(part * block, block)

    def read(g):
        slot = lax.rem(g, depth)
        here = pl.ds(first + g * group, group)
        return [
            pltpu.make_async_copy(ref.at[here], blocks.at[slot, n], a_sems.at[slot, n])
            for n, ref in enumerate((own_ref, other_ref))
        ]

    def write(g):
        slot = lax.rem(g, 2)
        return pltpu.make_async_copy(
            sums.at[slot], out_ref.at[:, pl.ds(g * group, group)], out_sems.at[slot]
        )

    copies = []
    for p, ref in enumerate(v_refs):
        rows = ref.shape[0]
        target = v_all.at[place(p, rows, parts[p])]
        copies.append(pltpu.make_async_copy(ref, target, v_sems.at[p]))
    for copy in copies:
        copy.start()
    for g in range(depth - 1):
        for copy in read(g):
            copy.start()
    for n, (rows, part) in enumerate(fills):
        at = place(pieces + n, rows, part)
        v_all[at] = jnp.zeros((rows, block), v_all.dtype)
    for copy in copies:
        copy.wait()

    def one(g, carry):
        slot, out_slot = lax.rem(g, depth), lax.rem(g, 2)

        @pl.when(g + depth - 1 < groups)
        def _():
            for copy in read(g + depth - 1):
                copy.start()

        for copy in read(g):
            copy.wait()

        @pl.when(g >= 2)
        def _():
            write(g - 2).wait()

        for r in range(group):
            left, right = [], []
            for n in range(2):
                for s in range(slots):
                    code = cols_ref[first + g * group + r, n * slots + s]
                    left.append(blocks[slot, n, r, s])
                    right.append(v_all[pl.ds(pl.multiple_of(code * block, block), block), :])
            product = jnp.dot(
                jnp.concatenate(left, axis=1),
                jnp.concatenate(right, axis=0),
                preferred_element_type=jnp.float32,
            )
            for part in range(2):
                sums[out_slot, part, r] = product[:, part * block : (part + 1) * block]
        write(g).start()
        return carry

    lax.fori_loop(0, groups, one, 0)
    for g in range(max(groups - 2, 0), groups):
        write(g).wait()


def image_of(cols, own, other, v_pieces, places, parts, fills, start, count):
    rows, slots, block = own.shape[:3]
    group = largest_divisor(count, 4)
    depth = min(3, count // group + 1)
    pieces = len(v_pieces)
    offs = jnp.stack([*places, *[f[0] for f in fills], start]).astype(jnp.int32)
    fill_shapes = tuple((f[1] * block, f[2]) for f in fills)
    return pl.pallas_call(
        functools.partial(image_kernel, group, parts, fill_shapes),
        out_shape=jax.ShapeDtypeStruct((2, count, block, block), jnp.float32),
        grid_spec=pltpu.PrefetchScalarGridSpec(
            num_scalar_prefetch=2,
            grid=(1,),
            in_specs=anywhere(2 + pieces),
            out_specs=pl.BlockSpec(memory_space=pl.ANY),
            scratch_shapes=[
                pltpu.VMEM((3 * rows * block, 2 * block), jnp.bfloat16),
                pltpu.VMEM((depth, 2, group, slots, block, block), jnp.bfloat16),
                pltpu.VMEM((2, 2, group, block, block), jnp.float32),
                pltpu.SemaphoreType.DMA((pieces,)),
                pltpu.SemaphoreType.DMA((depth, 2)),
                pltpu.SemaphoreType.DMA((2,)),
            ],
        ),
        compiler_params=pltpu.CompilerParams(vmem_limit_bytes=VMEM),
        cost_estimate=SMALL,
        name="image",
    )(cols, offs, own, other, *v_pieces)


def cut_kernel(start_ref, v_ref, out_ref, stage, sems):
    start = pl.multiple_of(start_ref[0] * 128, 128)
    read = pltpu.make_async_copy(v_ref.at[pl.ds(start, stage.shape[0])], stage, sems.at[0])
    write = pltpu.make_async_copy(stage, out_ref, sems.at[1])
    read.start()
    read.wait()
    write.start()
    write.wait()


def cut(array, start, length):
    part = jax.ShapeDtypeStruct((length, array.shape[1]), array.dtype)
    return pl.pallas_call(
        cut_kernel,
        out_shape=part,
        grid_spec=pltpu.PrefetchScalarGridSpec(
            num_scalar_prefetch=1,
            grid=(1,),
            in_specs=anywhere(1),
            out_specs=pl.BlockSpec(memory_space=pl.ANY),
            scratch_shapes=[pltpu.VMEM(part.shape, part.dtype), pltpu.SemaphoreType.DMA((2,))],
        ),
        cost_estimate=SMALL,
        name="cut",
    )(jnp.reshape(start, (1,)).astype(jnp.int32), array)


def lists_kernel(rows, slots, plan, codes_ref, *refs):
    outs, steps_ref = refs[:-1], refs[-1]
    per_source = LANES * PAIR
    size = 2 * rows * slots
    lengths = [out.shape[0] // 2 for out in outs]
    turns = max(len(classes) for classes in plan)

    def one_row(row, ends):
        ends = list(ends)
        for turn in range(turns):
            active = [
                (2 * k + source, out, classes[turn] * size + (source * rows + row) * slots)
                for k, (out, classes) in enumerate(zip(outs, plan))
                if turn < len(classes)
                for source in range(2)
            ]
            for s in range(slots):
                for n, out, base in active:
                    code = codes_ref[base + s]
                    out[ends[n]] = code
                    ends[n] = ends[n] + jnp.minimum(code, 1)
            for n, out, _ in active:
                out[ends[n]] = 0
                ends[n] = ends[n] + (ends[n] & (PAIR - 1))
        return tuple(ends)

    first = tuple(jnp.int32(source * length) for length in lengths for source in range(2))
    ends = lax.fori_loop(0, rows, one_row, first)
    for k, out in enumerate(outs):
        pair = ends[2 * k], ends[2 * k + 1]
        most = jnp.maximum(pair[0], pair[1] - lengths[k])
        steps = lax.div(most + per_source - 1, per_source)
        steps_ref[k] = steps
        for source in range(2):
            def clear(at, carry, out=out):
                out[at] = 0
                return carry

            lax.fori_loop(pair[source], source * lengths[k] + steps * per_source, clear, 0)


def lists_of(codes, rows, slots, plan):
    lengths = [2 * capacity_of(rows, slots, len(c)) * PAIR for c in plan]
    smem = pl.BlockSpec(memory_space=pltpu.SMEM)
    *lists, steps = pl.pallas_call(
        functools.partial(lists_kernel, rows, slots, plan),
        out_shape=[jax.ShapeDtypeStruct((n,), jnp.int32) for n in lengths + [len(plan)]],
        in_specs=[smem],
        out_specs=[smem] * (len(plan) + 1),
        cost_estimate=SMALL,
        name="lists",
    )(codes)
    return lists, steps


def capacity_of(rows, slots, parts):
    tasks = (rows * slots + rows * parts * (PAIR - 1)) // PAIR
    return (-(-tasks // LANES) + 1) * LANES


def add_listed(codes_ref, steps, a_refs, v_all, blocks, sems, total):
    block = blocks.shape[-1]
    per_source = LANES * PAIR
    length = codes_ref.shape[0] // len(a_refs)

    def fetch(step):
        slot = lax.rem(step, DEPTH)
        for s, a_ref in enumerate(a_refs):
            for n in range(per_source):
                code = codes_ref[s * length + step * per_source + n]
                block_id = (code >> V_BITS) & ((1 << BLOCK_BITS) - 1)
                pltpu.make_async_copy(
                    a_ref.at[block_id], blocks.at[slot, s * per_source + n], sems.at[slot]
                ).start()

    for ahead in range(DEPTH - 1):
        @pl.when(ahead < steps)
        def _():
            fetch(ahead)

    def run():
        def one(step, carry):
            slot = lax.rem(step, DEPTH)

            @pl.when(step + DEPTH - 1 < steps)
            def _():
                fetch(step + DEPTH - 1)

            pltpu.make_async_copy(blocks.at[slot], blocks.at[slot], sems.at[slot]).wait()
            products = []
            for s in range(len(a_refs)):
                for n in range(LANES):
                    left, right = [], []
                    for g in range(PAIR):
                        at = n * PAIR + g
                        code = codes_ref[s * length + step * per_source + at]
                        if g == 0:
                            row = code >> (BLOCK_BITS + V_BITS)
                        start = pl.multiple_of((code & ((1 << V_BITS) - 1)) * block, block)
                        left.append(blocks[slot, s * per_source + at])
                        right.append(v_all[pl.ds(start, block), :])
                    product = jnp.dot(
                        jnp.concatenate(left, axis=1),
                        jnp.concatenate(right, axis=0),
                        preferred_element_type=jnp.float32,
                    )
                    products.append((row, product))
            for row, product in products:
                total[row] += product
            return carry

        lax.fori_loop(0, steps, one, 0)

    return run


def list_scratch(v_pieces, block):
    v_rows = block + sum(v.shape[0] for v in v_pieces)
    return [
        pltpu.VMEM((v_rows, block), jnp.bfloat16),
        pltpu.VMEM((DEPTH, 2 * LANES * PAIR, block, block), jnp.bfloat16),
        pltpu.SemaphoreType.DMA((DEPTH,)),
    ]


def copies_of(pairs, sems):
    copies = [pltpu.make_async_copy(a, b, sems.at[n]) for n, (a, b) in enumerate(pairs)]
    for copy in copies:
        copy.start()
    return copies


def v_places(v_refs, v_all, block):
    places, at = [], block
    for ref in v_refs:
        places.append((ref, v_all.at[pl.ds(at, ref.shape[0])]))
        at += ref.shape[0]
    return places


def later_kernel(pieces, codes_ref, steps_ref, me_ref, own_ref, other_ref, *refs):
    images, v_refs, refs = refs[:2], refs[2 : 2 + pieces], refs[2 + pieces :]
    out_ref, v_all, blocks, a_sems, sems = refs
    block = out_ref.shape[1]
    pairs = v_places(v_refs, v_all, block)
    for n, ref in enumerate(images):
        pairs.append((ref.at[1], out_ref.at[pl.ds(me_ref[1 + n], ref.shape[1])]))
    copies = copies_of(pairs, sems)
    run = add_listed(
        codes_ref, steps_ref[0], (own_ref, other_ref), v_all, blocks, a_sems, out_ref
    )
    v_all[pl.ds(0, block), :] = jnp.zeros((block, block), v_all.dtype)
    for copy in copies:
        copy.wait()
    run()


def later_image(codes, steps, me, own, other, images, v_pieces):
    block = own.shape[-1]
    shape = (sum(image.shape[1] for image in images), block, block)
    return pl.pallas_call(
        functools.partial(later_kernel, len(v_pieces)),
        out_shape=jax.ShapeDtypeStruct(shape, jnp.float32),
        grid_spec=pltpu.PrefetchScalarGridSpec(
            num_scalar_prefetch=3,
            grid=(1,),
            in_specs=anywhere(4 + len(v_pieces)),
            out_specs=pl.BlockSpec(shape, lambda i, *_: (0, 0, 0)),
            scratch_shapes=list_scratch(v_pieces, block)
            + [pltpu.SemaphoreType.DMA((len(v_pieces) + 2,))],
        ),
        compiler_params=pltpu.CompilerParams(vmem_limit_bytes=VMEM),
        cost_estimate=LARGE,
        name="later",
    )(codes, steps, me, own, other, *images, *v_pieces)


def last_kernel(pieces, codes_ref, steps_ref, me_ref, own_ref, other_ref, *refs):
    images, late_ref, refs = refs[:2], refs[2], refs[3:]
    v_refs, w_refs = refs[:pieces], refs[pieces : 4 + pieces]
    out_ref, v_all, blocks, a_sems, image, w_all, sems = refs[4 + pieces :]
    _, rows, block, _ = image.shape
    early = copies_of(v_places(v_refs, v_all, block) + [(late_ref, image.at[1])], sems)
    run = add_listed(
        codes_ref, steps_ref[1], (own_ref, other_ref), v_all, blocks, a_sems, image.at[1]
    )
    w_places = [(w_refs[q], w_all.at[q]) for q in range(4)]
    for n, ref in enumerate(images):
        w_places.append((ref.at[0], image.at[0, pl.ds(me_ref[1 + n], ref.shape[1])]))
    later = copies_of(w_places, sems.at[pl.ds(pieces + 1, 6)])
    v_all[pl.ds(0, block), :] = jnp.zeros((block, block), v_all.dtype)
    for copy in early:
        copy.wait()
    run()
    for copy in later:
        copy.wait()
    length = rows // 4
    total = None
    for q in range(4):
        terms = []
        for part in range(2):
            here = image[part, pl.ds((me_ref[0] ^ q) * length, length)]
            here = here.reshape(length * block, block)
            upper = here.astype(jnp.bfloat16)
            terms += [upper, (here - upper.astype(jnp.float32)).astype(jnp.bfloat16)]
        term = jnp.dot(
            w_all[q], jnp.concatenate(terms, axis=1), preferred_element_type=jnp.float32
        )
        total = term if total is None else total + term
    mine = me_ref[0] >> 1
    count, _, tile, _ = out_ref.shape
    for part, place in ((0, mine), (1, 1 - mine)):
        first = 2 * part * block
        both = total[:, first : first + block] + total[:, first + block : first + 2 * block]
        out_ref[:, place] = both.reshape(count, tile, block)


def last_projected(codes, steps, me, own, other, images, late, v_pieces, w_pieces, devices):
    rows, block, _ = late.shape
    basis, length = w_pieces[0].shape
    shape = (devices, 2, basis // devices, block)
    return pl.pallas_call(
        functools.partial(last_kernel, len(v_pieces)),
        out_shape=jax.ShapeDtypeStruct(shape, jnp.float32),
        grid_spec=pltpu.PrefetchScalarGridSpec(
            num_scalar_prefetch=3,
            grid=(1,),
            in_specs=anywhere(9 + len(v_pieces)),
            out_specs=pl.BlockSpec(shape, lambda i, *_: (0, 0, 0, 0)),
            scratch_shapes=list_scratch(v_pieces, block)
            + [
                pltpu.VMEM((2, rows, block, block), jnp.float32),
                pltpu.VMEM((4, basis, length), jnp.bfloat16),
                pltpu.SemaphoreType.DMA((len(v_pieces) + 7,)),
            ],
        ),
        compiler_params=pltpu.CompilerParams(vmem_limit_bytes=VMEM),
        cost_estimate=SMALL,
        name="last_projected",
    )(codes, steps, me, own, other, *images, late, *v_pieces, *w_pieces)


def shards(basis_v, basis_w, couplings, coupling_cols):
    rows, slots, block = couplings.shape[:3]
    regions, columns = lax.axis_size("region"), lax.axis_size("col")
    region, col = lax.axis_index("region"), lax.axis_index("col")
    odd = region % 2
    half = rows // 2

    own_a = cut(basis_v, odd * half, half * block)
    near_a, side_a = to_near(own_a), to_side(own_a)
    here = after(coupling_cols, own_a) - (region * rows - rows)
    there = to_core(here)
    other = to_core(after(couplings, there))
    own_b = cut(after(basis_v, there), (1 - odd) * half, half * block)
    near_b, side_b = to_near(own_b), to_side(own_b)
    w_own = basis_w.T

    cols = jnp.concatenate([here, there], axis=1)
    near_base = jnp.where(odd == 1, 0, 2 * rows)
    far_base = 2 * rows - near_base
    first, second = (1 - odd) * half, odd * half
    near_at = [near_base + first, near_base + second]
    far_at = [far_base + first, far_base + second]
    own_at = [rows + second, rows + first]
    me = jnp.stack([col, first, second]).astype(jnp.int32)

    both = jnp.stack([here, there])[None]
    in_near = both // rows == near_base // rows
    in_far = both // rows == far_base // rows
    is_a = (both % rows >= half) == (odd == 0)
    kind = jnp.arange(2, dtype=jnp.int32)[:, None, None, None]
    row = jnp.arange(rows, dtype=jnp.int32)[:, None]
    summed_early = (row >= half) == (odd == 0)
    taken = jnp.where(
        kind == 0, (in_near & (~is_a | summed_early)) | (in_far & is_a), in_far & ~is_a
    )
    piece = jnp.where(kind == 0, jnp.where(in_far, 2, jnp.where(is_a, 0, 1)), 0)
    block_id = row * slots + jnp.arange(slots, dtype=jnp.int32)[None, :]
    codes = (row << (BLOCK_BITS + V_BITS)) + (block_id << V_BITS)
    codes = jnp.where(taken, codes + 1 + piece * half + both % half, 0).reshape(-1)
    (later, last), steps = lists_of(codes, rows, slots, ((0,), (1,)))

    near_a, side_a, steps, cols, me, w_own = together(near_a, side_a, steps, cols, me, w_own)
    far_a, near_side_a = onward(near_a), to_near(side_a)

    near_b, side_b, other = together(near_b, side_b, other)
    far_b, near_side_b = onward(after(near_b, far_a)), to_near(side_b)
    w_side = to_side(after(w_own, near_b))
    pieces = [basis_v, near_a, near_b, far_a, side_a, side_b]
    at = [jnp.int32(rows), *near_at, far_at[0], *own_at]
    fills = [(far_at[1], half, 0), (near_base, rows, 1), (far_base, rows, 1)]
    early = image_of(
        cols, couplings, other, pieces, at, (0, 0, 0, 0, 1, 1), fills, first, half
    )

    early, near_side_a = together(early, near_side_a)
    far_side_a = onward(near_side_a)
    pieces = [basis_v, near_a, near_b, far_a, far_b, side_a, side_b, near_side_a]
    at = [jnp.int32(rows), *near_at, *far_at, *own_at, near_at[0]]
    fills = [(near_at[1], half, 1), (far_base, rows, 1)]
    rest = image_of(
        cols, couplings, other, pieces, at, (0, 0, 0, 0, 0, 1, 1, 1), fills, second, half
    )
    images = [early, rest]
    rest, side_b, w_own, w_side = together(rest, side_b, w_own, w_side)
    far_side_b = to_far(side_b)
    w_pieces = [w_own, to_core(w_own), w_side, to_core(w_side)]
    images = [early, rest]
    own_list = couplings.reshape(rows * slots, block, block)
    other_list = other.reshape(rows * slots, block, block)
    pieces = [near_side_a, near_side_b, far_side_a]
    image = later_image(later, steps, me, own_list, other_list, images, pieces)

    sent = last_projected(
        last, steps, me, own_list, other_list, images, image, [far_side_b], w_pieces,
        regions * columns,
    )
    received = lax.all_to_all(sent, EVERY, 0, 0, tiled=True)
    tile = sent.shape[2]
    summed = received.reshape(regions, columns // 2, 2, 2, tile, block).sum(axis=(0, 1))
    return summed.transpose(2, 1, 0, 3).reshape(tile, columns * block)


def solution(mesh):
    in_specs = (
        P("region", "col"),
        P(("region", "col"), None),
        P("region", "col", None, None),
        P("region", "col"),
    )
    out_specs = P(("region", "col"), None)
    return jax.shard_map(shards, mesh=mesh, in_specs=in_specs, out_specs=out_specs, check_vma=False)
```

```python
import functools

import jax
import jax.numpy as jnp
from jax import lax
from jax.experimental import pallas as pl
from jax.experimental.pallas import tpu as pltpu
from jax.sharding import PartitionSpec as P

EVERY = ("region", "col")
VMEM = 34 * 2**20
PAIR = 2
LANES = 8
DEPTH = 5
V_BITS, BLOCK_BITS = 8, 10
SMALL = pl.CostEstimate(flops=1, bytes_accessed=1, transcendentals=0)
LARGE = pl.CostEstimate(flops=10**12, bytes_accessed=10**9, transcendentals=0)


def moved(array, axis, target):
    count = lax.axis_size(axis)
    pairs = [(i, target(i)) for i in range(count)]
    return lax.ppermute(array, axis, [(i, j) for i, j in pairs if 0 <= j < count])


def to_core(array):
    return moved(array, "col", lambda c: c ^ 1)


def to_side(array):
    return moved(array, "col", lambda c: c ^ 2)


def to_near(array):
    return moved(array, "region", lambda r: r ^ 1)


def to_far(array):
    return moved(array, "region", lambda r: r + 1 if r % 2 else r - 1)


def onward(array):
    return moved(array, "region", lambda r: r - 2 if r % 2 else r + 2)


def together(*arrays):
    return lax.optimization_barrier(arrays)


def after(array, *others):
    return together(array, *others)[0]


def largest_divisor(length, limit):
    return max(d for d in range(1, limit + 1) if length % d == 0)


def anywhere(count):
    return [pl.BlockSpec(memory_space=pl.ANY)] * count


def image_kernel(group, parts, fills, cols_ref, offs_ref, own_ref, other_ref, *refs):
    pieces = len(parts)
    v_refs, refs = refs[:pieces], refs[pieces:]
    out_ref, v_all, blocks, sums, v_sems, a_sems, out_sems = refs
    depth, _, _, slots, block, _ = blocks.shape
    count = out_ref.shape[1]
    groups = count // group
    first = offs_ref[pieces + len(fills)]

    def place(n, rows, part):
        start = pl.multiple_of(offs_ref[n] * block, block)
        return pl.ds(start, rows), pl.ds(part * block, block)

    def read(g):
        slot = lax.rem(g, depth)
        here = pl.ds(first + g * group, group)
        return [
            pltpu.make_async_copy(ref.at[here], blocks.at[slot, n], a_sems.at[slot, n])
            for n, ref in enumerate((own_ref, other_ref))
        ]

    def write(g):
        slot = lax.rem(g, 2)
        return pltpu.make_async_copy(
            sums.at[slot], out_ref.at[:, pl.ds(g * group, group)], out_sems.at[slot]
        )

    copies = []
    for p, ref in enumerate(v_refs):
        rows = ref.shape[0]
        target = v_all.at[place(p, rows, parts[p])]
        copies.append(pltpu.make_async_copy(ref, target, v_sems.at[p]))
    for copy in copies:
        copy.start()
    for g in range(depth - 1):
        for copy in read(g):
            copy.start()
    for n, (rows, part) in enumerate(fills):
        at = place(pieces + n, rows, part)
        v_all[at] = jnp.zeros((rows, block), v_all.dtype)
    for copy in copies:
        copy.wait()

    def one(g, carry):
        slot, out_slot = lax.rem(g, depth), lax.rem(g, 2)

        @pl.when(g + depth - 1 < groups)
        def _():
            for copy in read(g + depth - 1):
                copy.start()

        for copy in read(g):
            copy.wait()

        @pl.when(g >= 2)
        def _():
            write(g - 2).wait()

        for r in range(group):
            left, right = [], []
            for n in range(2):
                for s in range(slots):
                    code = cols_ref[first + g * group + r, n * slots + s]
                    left.append(blocks[slot, n, r, s])
                    right.append(v_all[pl.ds(pl.multiple_of(code * block, block), block), :])
            product = jnp.dot(
                jnp.concatenate(left, axis=1),
                jnp.concatenate(right, axis=0),
                preferred_element_type=jnp.float32,
            )
            for part in range(2):
                sums[out_slot, part, r] = product[:, part * block : (part + 1) * block]
        write(g).start()
        return carry

    lax.fori_loop(0, groups, one, 0)
    for g in range(max(groups - 2, 0), groups):
        write(g).wait()


def image_of(cols, own, other, v_pieces, places, parts, fills, start, count):
    rows, slots, block = own.shape[:3]
    group = largest_divisor(count, 4)
    depth = min(3, count // group + 1)
    pieces = len(v_pieces)
    offs = jnp.stack([*places, *[f[0] for f in fills], start]).astype(jnp.int32)
    fill_shapes = tuple((f[1] * block, f[2]) for f in fills)
    return pl.pallas_call(
        functools.partial(image_kernel, group, parts, fill_shapes),
        out_shape=jax.ShapeDtypeStruct((2, count, block, block), jnp.float32),
        grid_spec=pltpu.PrefetchScalarGridSpec(
            num_scalar_prefetch=2,
            grid=(1,),
            in_specs=anywhere(2 + pieces),
            out_specs=pl.BlockSpec(memory_space=pl.ANY),
            scratch_shapes=[
                pltpu.VMEM((3 * rows * block, 2 * block), jnp.bfloat16),
                pltpu.VMEM((depth, 2, group, slots, block, block), jnp.bfloat16),
                pltpu.VMEM((2, 2, group, block, block), jnp.float32),
                pltpu.SemaphoreType.DMA((pieces,)),
                pltpu.SemaphoreType.DMA((depth, 2)),
                pltpu.SemaphoreType.DMA((2,)),
            ],
        ),
        compiler_params=pltpu.CompilerParams(vmem_limit_bytes=VMEM),
        cost_estimate=SMALL,
        name="image",
    )(cols, offs, own, other, *v_pieces)


def cut_kernel(start_ref, v_ref, out_ref, stage, sems):
    start = pl.multiple_of(start_ref[0] * 128, 128)
    read = pltpu.make_async_copy(v_ref.at[pl.ds(start, stage.shape[0])], stage, sems.at[0])
    write = pltpu.make_async_copy(stage, out_ref, sems.at[1])
    read.start()
    read.wait()
    write.start()
    write.wait()


def cut(array, start, length):
    part = jax.ShapeDtypeStruct((length, array.shape[1]), array.dtype)
    return pl.pallas_call(
        cut_kernel,
        out_shape=part,
        grid_spec=pltpu.PrefetchScalarGridSpec(
            num_scalar_prefetch=1,
            grid=(1,),
            in_specs=anywhere(1),
            out_specs=pl.BlockSpec(memory_space=pl.ANY),
            scratch_shapes=[pltpu.VMEM(part.shape, part.dtype), pltpu.SemaphoreType.DMA((2,))],
        ),
        cost_estimate=SMALL,
        name="cut",
    )(jnp.reshape(start, (1,)).astype(jnp.int32), array)


def lists_kernel(rows, slots, plan, codes_ref, *refs):
    outs, steps_ref = refs[:-1], refs[-1]
    per_source = LANES * PAIR
    size = 2 * rows * slots
    lengths = [out.shape[0] // 2 for out in outs]
    turns = max(len(classes) for classes in plan)

    def one_row(row, ends):
        ends = list(ends)
        for turn in range(turns):
            active = [
                (2 * k + source, out, classes[turn] * size + (source * rows + row) * slots)
                for k, (out, classes) in enumerate(zip(outs, plan))
                if turn < len(classes)
                for source in range(2)
            ]
            for s in range(slots):
                for n, out, base in active:
                    code = codes_ref[base + s]
                    out[ends[n]] = code
                    ends[n] = ends[n] + jnp.minimum(code, 1)
            for n, out, _ in active:
                out[ends[n]] = 0
                ends[n] = ends[n] + (ends[n] & (PAIR - 1))
        return tuple(ends)

    first = tuple(jnp.int32(source * length) for length in lengths for source in range(2))
    ends = lax.fori_loop(0, rows, one_row, first)
    for k, out in enumerate(outs):
        pair = ends[2 * k], ends[2 * k + 1]
        most = jnp.maximum(pair[0], pair[1] - lengths[k])
        steps = lax.div(most + per_source - 1, per_source)
        steps_ref[k] = steps
        for source in range(2):
            def clear(at, carry, out=out):
                out[at] = 0
                return carry

            lax.fori_loop(pair[source], source * lengths[k] + steps * per_source, clear, 0)


def lists_of(codes, rows, slots, plan):
    lengths = [2 * capacity_of(rows, slots, len(c)) * PAIR for c in plan]
    smem = pl.BlockSpec(memory_space=pltpu.SMEM)
    *lists, steps = pl.pallas_call(
        functools.partial(lists_kernel, rows, slots, plan),
        out_shape=[jax.ShapeDtypeStruct((n,), jnp.int32) for n in lengths + [len(plan)]],
        in_specs=[smem],
        out_specs=[smem] * (len(plan) + 1),
        cost_estimate=SMALL,
        name="lists",
    )(codes)
    return lists, steps


def capacity_of(rows, slots, parts):
    tasks = (rows * slots + rows * parts * (PAIR - 1)) // PAIR
    return (-(-tasks // LANES) + 1) * LANES


def add_listed(codes_ref, steps, a_refs, v_all, blocks, sems, total):
    block = blocks.shape[-1]
    per_source = LANES * PAIR
    length = codes_ref.shape[0] // len(a_refs)

    def fetch(step):
        slot = lax.rem(step, DEPTH)
        for s, a_ref in enumerate(a_refs):
            for n in range(per_source):
                code = codes_ref[s * length + step * per_source + n]
                block_id = (code >> V_BITS) & ((1 << BLOCK_BITS) - 1)
                pltpu.make_async_copy(
                    a_ref.at[block_id], blocks.at[slot, s * per_source + n], sems.at[slot]
                ).start()

    for ahead in range(DEPTH - 1):
        @pl.when(ahead < steps)
        def _():
            fetch(ahead)

    def run():
        def one(step, carry):
            slot = lax.rem(step, DEPTH)

            @pl.when(step + DEPTH - 1 < steps)
            def _():
                fetch(step + DEPTH - 1)

            pltpu.make_async_copy(blocks.at[slot], blocks.at[slot], sems.at[slot]).wait()
            products = []
            for s in range(len(a_refs)):
                for n in range(LANES):
                    left, right = [], []
                    for g in range(PAIR):
                        at = n * PAIR + g
                        code = codes_ref[s * length + step * per_source + at]
                        if g == 0:
                            row = code >> (BLOCK_BITS + V_BITS)
                        start = pl.multiple_of((code & ((1 << V_BITS) - 1)) * block, block)
                        left.append(blocks[slot, s * per_source + at])
                        right.append(v_all[pl.ds(start, block), :])
                    product = jnp.dot(
                        jnp.concatenate(left, axis=1),
                        jnp.concatenate(right, axis=0),
                        preferred_element_type=jnp.float32,
                    )
                    products.append((row, product))
            for row, product in products:
                total[row] += product
            return carry

        lax.fori_loop(0, steps, one, 0)

    return run


def list_scratch(v_pieces, block):
    v_rows = block + sum(v.shape[0] for v in v_pieces)
    return [
        pltpu.VMEM((v_rows, block), jnp.bfloat16),
        pltpu.VMEM((DEPTH, 2 * LANES * PAIR, block, block), jnp.bfloat16),
        pltpu.SemaphoreType.DMA((DEPTH,)),
    ]


def copies_of(pairs, sems):
    copies = [pltpu.make_async_copy(a, b, sems.at[n]) for n, (a, b) in enumerate(pairs)]
    for copy in copies:
        copy.start()
    return copies


def v_places(v_refs, v_all, block):
    places, at = [], block
    for ref in v_refs:
        places.append((ref, v_all.at[pl.ds(at, ref.shape[0])]))
        at += ref.shape[0]
    return places


def later_kernel(pieces, codes_ref, steps_ref, me_ref, own_ref, other_ref, *refs):
    images, v_refs, refs = refs[:2], refs[2 : 2 + pieces], refs[2 + pieces :]
    out_ref, v_all, blocks, a_sems, sems = refs
    block = out_ref.shape[1]
    pairs = v_places(v_refs, v_all, block)
    for n, ref in enumerate(images):
        pairs.append((ref.at[1], out_ref.at[pl.ds(me_ref[1 + n], ref.shape[1])]))
    copies = copies_of(pairs, sems)
    run = add_listed(
        codes_ref, steps_ref[0], (own_ref, other_ref), v_all, blocks, a_sems, out_ref
    )
    v_all[pl.ds(0, block), :] = jnp.zeros((block, block), v_all.dtype)
    for copy in copies:
        copy.wait()
    run()


def later_image(codes, steps, me, own, other, images, v_pieces):
    block = own.shape[-1]
    shape = (sum(image.shape[1] for image in images), block, block)
    return pl.pallas_call(
        functools.partial(later_kernel, len(v_pieces)),
        out_shape=jax.ShapeDtypeStruct(shape, jnp.float32),
        grid_spec=pltpu.PrefetchScalarGridSpec(
            num_scalar_prefetch=3,
            grid=(1,),
            in_specs=anywhere(4 + len(v_pieces)),
            out_specs=pl.BlockSpec(shape, lambda i, *_: (0, 0, 0)),
            scratch_shapes=list_scratch(v_pieces, block)
            + [pltpu.SemaphoreType.DMA((len(v_pieces) + 2,))],
        ),
        compiler_params=pltpu.CompilerParams(vmem_limit_bytes=VMEM),
        cost_estimate=LARGE,
        name="later",
    )(codes, steps, me, own, other, *images, *v_pieces)


def last_kernel(pieces, codes_ref, steps_ref, me_ref, own_ref, other_ref, *refs):
    images, late_ref, refs = refs[:2], refs[2], refs[3:]
    v_refs, w_refs = refs[:pieces], refs[pieces : 4 + pieces]
    out_ref, v_all, blocks, a_sems, image, w_all, sems = refs[4 + pieces :]
    _, rows, block, _ = image.shape
    early = copies_of(v_places(v_refs, v_all, block) + [(late_ref, image.at[1])], sems)
    run = add_listed(
        codes_ref, steps_ref[1], (own_ref, other_ref), v_all, blocks, a_sems, image.at[1]
    )
    w_places = [(w_refs[q], w_all.at[q]) for q in range(4)]
    for n, ref in enumerate(images):
        w_places.append((ref.at[0], image.at[0, pl.ds(me_ref[1 + n], ref.shape[1])]))
    later = copies_of(w_places, sems.at[pl.ds(pieces + 1, 6)])
    v_all[pl.ds(0, block), :] = jnp.zeros((block, block), v_all.dtype)
    for copy in early:
        copy.wait()
    run()
    for copy in later:
        copy.wait()
    length = rows // 4
    total = None
    for q in range(4):
        terms = []
        for part in range(2):
            here = image[part, pl.ds((me_ref[0] ^ q) * length, length)]
            here = here.reshape(length * block, block)
            upper = here.astype(jnp.bfloat16)
            terms += [upper, (here - upper.astype(jnp.float32)).astype(jnp.bfloat16)]
        term = jnp.dot(
            w_all[q], jnp.concatenate(terms, axis=1), preferred_element_type=jnp.float32
        )
        total = term if total is None else total + term
    mine = me_ref[0] >> 1
    count, _, tile, _ = out_ref.shape
    for part, place in ((0, mine), (1, 1 - mine)):
        first = 2 * part * block
        both = total[:, first : first + block] + total[:, first + block : first + 2 * block]
        out_ref[:, place] = both.reshape(count, tile, block)


def last_projected(codes, steps, me, own, other, images, late, v_pieces, w_pieces, devices):
    rows, block, _ = late.shape
    basis, length = w_pieces[0].shape
    shape = (devices, 2, basis // devices, block)
    return pl.pallas_call(
        functools.partial(last_kernel, len(v_pieces)),
        out_shape=jax.ShapeDtypeStruct(shape, jnp.float32),
        grid_spec=pltpu.PrefetchScalarGridSpec(
            num_scalar_prefetch=3,
            grid=(1,),
            in_specs=anywhere(9 + len(v_pieces)),
            out_specs=pl.BlockSpec(shape, lambda i, *_: (0, 0, 0, 0)),
            scratch_shapes=list_scratch(v_pieces, block)
            + [
                pltpu.VMEM((2, rows, block, block), jnp.float32),
                pltpu.VMEM((4, basis, length), jnp.bfloat16),
                pltpu.SemaphoreType.DMA((len(v_pieces) + 7,)),
            ],
        ),
        compiler_params=pltpu.CompilerParams(vmem_limit_bytes=VMEM),
        cost_estimate=SMALL,
        name="last_projected",
    )(codes, steps, me, own, other, *images, late, *v_pieces, *w_pieces)


def shards(basis_v, basis_w, couplings, coupling_cols):
    rows, slots, block = couplings.shape[:3]
    regions, columns = lax.axis_size("region"), lax.axis_size("col")
    region, col = lax.axis_index("region"), lax.axis_index("col")
    odd = region % 2
    half = rows // 2

    own_a = cut(basis_v, odd * half, half * block)
    near_a, side_a = to_near(own_a), to_side(own_a)
    here = after(coupling_cols, own_a) - (region * rows - rows)
    there = to_core(here)
    other = to_core(after(couplings, there))
    own_b = cut(after(basis_v, there), (1 - odd) * half, half * block)
    near_b, side_b = to_near(own_b), to_side(own_b)
    w_own = basis_w.T

    cols = jnp.concatenate([here, there], axis=1)
    near_base = jnp.where(odd == 1, 0, 2 * rows)
    far_base = 2 * rows - near_base
    first, second = (1 - odd) * half, odd * half
    near_at = [near_base + first, near_base + second]
    far_at = [far_base + first, far_base + second]
    own_at = [rows + second, rows + first]
    me = jnp.stack([col, first, second]).astype(jnp.int32)

    both = jnp.stack([here, there])[None]
    in_near = both // rows == near_base // rows
    in_far = both // rows == far_base // rows
    is_a = (both % rows >= half) == (odd == 0)
    kind = jnp.arange(2, dtype=jnp.int32)[:, None, None, None]
    row = jnp.arange(rows, dtype=jnp.int32)[:, None]
    summed_early = (row >= half) == (odd == 0)
    taken = jnp.where(
        kind == 0, (in_near & (~is_a | summed_early)) | (in_far & is_a), in_far & ~is_a
    )
    piece = jnp.where(kind == 0, jnp.where(in_far, 2, jnp.where(is_a, 0, 1)), 0)
    block_id = row * slots + jnp.arange(slots, dtype=jnp.int32)[None, :]
    codes = (row << (BLOCK_BITS + V_BITS)) + (block_id << V_BITS)
    codes = jnp.where(taken, codes + 1 + piece * half + both % half, 0).reshape(-1)
    (later, last), steps = lists_of(codes, rows, slots, ((0,), (1,)))

    near_a, side_a, steps, cols, me, w_own = together(near_a, side_a, steps, cols, me, w_own)
    far_a, near_side_a = onward(near_a), to_near(side_a)

    near_b, side_b, other = together(near_b, side_b, other)
    far_b, near_side_b = onward(near_b), to_near(after(side_b, far_a))
    w_side = to_side(after(w_own, near_b))
    pieces = [basis_v, near_a, near_b, far_a, side_a, side_b]
    at = [jnp.int32(rows), *near_at, far_at[0], *own_at]
    fills = [(far_at[1], half, 0), (near_base, rows, 1), (far_base, rows, 1)]
    early = image_of(
        cols, couplings, other, pieces, at, (0, 0, 0, 0, 1, 1), fills, first, half
    )

    early, near_side_a = together(early, near_side_a)
    far_side_a = onward(near_side_a)
    pieces = [basis_v, near_a, near_b, far_a, far_b, side_a, side_b, near_side_a]
    at = [jnp.int32(rows), *near_at, *far_at, *own_at, near_at[0]]
    fills = [(near_at[1], half, 1), (far_base, rows, 1)]
    rest = image_of(
        cols, couplings, other, pieces, at, (0, 0, 0, 0, 0, 1, 1, 1), fills, second, half
    )
    images = [early, rest]
    rest, side_b, w_own, w_side = together(rest, side_b, w_own, w_side)
    far_side_b = to_far(side_b)
    w_pieces = [w_own, to_core(w_own), w_side, to_core(w_side)]
    images = [early, rest]
    own_list = couplings.reshape(rows * slots, block, block)
    other_list = other.reshape(rows * slots, block, block)
    pieces = [near_side_a, near_side_b, far_side_a]
    image = later_image(later, steps, me, own_list, other_list, images, pieces)

    sent = last_projected(
        last, steps, me, own_list, other_list, images, image, [far_side_b], w_pieces,
        regions * columns,
    )
    received = lax.all_to_all(sent, EVERY, 0, 0, tiled=True)
    tile = sent.shape[2]
    summed = received.reshape(regions, columns // 2, 2, 2, tile, block).sum(axis=(0, 1))
    return summed.transpose(2, 1, 0, 3).reshape(tile, columns * block)


def solution(mesh):
    in_specs = (
        P("region", "col"),
        P(("region", "col"), None),
        P("region", "col", None, None),
        P("region", "col"),
    )
    out_specs = P(("region", "col"), None)
    return jax.shard_map(shards, mesh=mesh, in_specs=in_specs, out_specs=out_specs, check_vma=False)
```

```python
import functools

import jax
import jax.numpy as jnp
from jax import lax
from jax.experimental import pallas as pl
from jax.experimental.pallas import tpu as pltpu
from jax.sharding import PartitionSpec as P

EVERY = ("region", "col")
VMEM = 34 * 2**20
PAIR = 2
LANES = 8
DEPTH = 5
V_BITS, BLOCK_BITS = 8, 10
SMALL = pl.CostEstimate(flops=1, bytes_accessed=1, transcendentals=0)
LARGE = pl.CostEstimate(flops=10**12, bytes_accessed=10**9, transcendentals=0)


def moved(array, axis, target):
    count = lax.axis_size(axis)
    pairs = [(i, target(i)) for i in range(count)]
    return lax.ppermute(array, axis, [(i, j) for i, j in pairs if 0 <= j < count])


def to_core(array):
    return moved(array, "col", lambda c: c ^ 1)


def to_side(array):
    return moved(array, "col", lambda c: c ^ 2)


def to_near(array):
    return moved(array, "region", lambda r: r ^ 1)


def beyond(array):
    return moved(array, "region", lambda r: r + 2 if r % 2 else r - 2)


def onward(array):
    return moved(array, "region", lambda r: r - 2 if r % 2 else r + 2)


def together(*arrays):
    return lax.optimization_barrier(arrays)


def after(array, *others):
    return together(array, *others)[0]


def largest_divisor(length, limit):
    return max(d for d in range(1, limit + 1) if length % d == 0)


def anywhere(count):
    return [pl.BlockSpec(memory_space=pl.ANY)] * count


def image_kernel(group, parts, fills, cols_ref, offs_ref, own_ref, other_ref, *refs):
    pieces = len(parts)
    v_refs, refs = refs[:pieces], refs[pieces:]
    out_ref, v_all, blocks, sums, v_sems, a_sems, out_sems = refs
    depth, _, _, slots, block, _ = blocks.shape
    count = out_ref.shape[1]
    groups = count // group
    first = offs_ref[pieces + len(fills)]

    def place(n, rows, part):
        start = pl.multiple_of(offs_ref[n] * block, block)
        return pl.ds(start, rows), pl.ds(part * block, block)

    def read(g):
        slot = lax.rem(g, depth)
        here = pl.ds(first + g * group, group)
        return [
            pltpu.make_async_copy(ref.at[here], blocks.at[slot, n], a_sems.at[slot, n])
            for n, ref in enumerate((own_ref, other_ref))
        ]

    def write(g):
        slot = lax.rem(g, 2)
        return pltpu.make_async_copy(
            sums.at[slot], out_ref.at[:, pl.ds(g * group, group)], out_sems.at[slot]
        )

    copies = []
    for p, ref in enumerate(v_refs):
        rows = ref.shape[0]
        target = v_all.at[place(p, rows, parts[p])]
        copies.append(pltpu.make_async_copy(ref, target, v_sems.at[p]))
    for copy in copies:
        copy.start()
    for g in range(depth - 1):
        for copy in read(g):
            copy.start()
    for n, (rows, part) in enumerate(fills):
        at = place(pieces + n, rows, part)
        v_all[at] = jnp.zeros((rows, block), v_all.dtype)
    for copy in copies:
        copy.wait()

    def one(g, carry):
        slot, out_slot = lax.rem(g, depth), lax.rem(g, 2)

        @pl.when(g + depth - 1 < groups)
        def _():
            for copy in read(g + depth - 1):
                copy.start()

        for copy in read(g):
            copy.wait()

        @pl.when(g >= 2)
        def _():
            write(g - 2).wait()

        for r in range(group):
            left, right = [], []
            for n in range(2):
                for s in range(slots):
                    code = cols_ref[first + g * group + r, n * slots + s]
                    left.append(blocks[slot, n, r, s])
                    right.append(v_all[pl.ds(pl.multiple_of(code * block, block), block), :])
            product = jnp.dot(
                jnp.concatenate(left, axis=1),
                jnp.concatenate(right, axis=0),
                preferred_element_type=jnp.float32,
            )
            for part in range(2):
                sums[out_slot, part, r] = product[:, part * block : (part + 1) * block]
        write(g).start()
        return carry

    lax.fori_loop(0, groups, one, 0)
    for g in range(max(groups - 2, 0), groups):
        write(g).wait()


def image_of(cols, own, other, v_pieces, places, parts, fills, start, count):
    rows, slots, block = own.shape[:3]
    group = largest_divisor(count, 4)
    depth = min(3, count // group + 1)
    pieces = len(v_pieces)
    offs = jnp.stack([*places, *[f[0] for f in fills], start]).astype(jnp.int32)
    fill_shapes = tuple((f[1] * block, f[2]) for f in fills)
    return pl.pallas_call(
        functools.partial(image_kernel, group, parts, fill_shapes),
        out_shape=jax.ShapeDtypeStruct((2, count, block, block), jnp.float32),
        grid_spec=pltpu.PrefetchScalarGridSpec(
            num_scalar_prefetch=2,
            grid=(1,),
            in_specs=anywhere(2 + pieces),
            out_specs=pl.BlockSpec(memory_space=pl.ANY),
            scratch_shapes=[
                pltpu.VMEM((3 * rows * block, 2 * block), jnp.bfloat16),
                pltpu.VMEM((depth, 2, group, slots, block, block), jnp.bfloat16),
                pltpu.VMEM((2, 2, group, block, block), jnp.float32),
                pltpu.SemaphoreType.DMA((pieces,)),
                pltpu.SemaphoreType.DMA((depth, 2)),
                pltpu.SemaphoreType.DMA((2,)),
            ],
        ),
        compiler_params=pltpu.CompilerParams(vmem_limit_bytes=VMEM),
        cost_estimate=SMALL,
        name="image",
    )(cols, offs, own, other, *v_pieces)


def cut_kernel(block, start_ref, v_ref, out_ref, stage, sems):
    start = pl.multiple_of(start_ref[0] * block, block)
    read = pltpu.make_async_copy(v_ref.at[pl.ds(start, stage.shape[0])], stage, sems.at[0])
    write = pltpu.make_async_copy(stage, out_ref, sems.at[1])
    read.start()
    read.wait()
    write.start()
    write.wait()


def cut(array, start, length, block):
    part = jax.ShapeDtypeStruct((length, array.shape[1]), array.dtype)
    return pl.pallas_call(
        functools.partial(cut_kernel, block),
        out_shape=part,
        grid_spec=pltpu.PrefetchScalarGridSpec(
            num_scalar_prefetch=1,
            grid=(1,),
            in_specs=anywhere(1),
            out_specs=pl.BlockSpec(memory_space=pl.ANY),
            scratch_shapes=[pltpu.VMEM(part.shape, part.dtype), pltpu.SemaphoreType.DMA((2,))],
        ),
        cost_estimate=SMALL,
        name="cut",
    )(jnp.reshape(start, (1,)).astype(jnp.int32), array)


def lists_kernel(rows, slots, plan, codes_ref, *refs):
    outs, steps_ref = refs[:-1], refs[-1]
    per_source = LANES * PAIR
    size = 2 * rows * slots
    lengths = [out.shape[0] // 2 for out in outs]
    turns = max(len(classes) for classes in plan)

    def one_row(row, ends):
        ends = list(ends)
        for turn in range(turns):
            active = [
                (2 * k + source, out, classes[turn] * size + (source * rows + row) * slots)
                for k, (out, classes) in enumerate(zip(outs, plan))
                if turn < len(classes)
                for source in range(2)
            ]
            for s in range(slots):
                for n, out, base in active:
                    code = codes_ref[base + s]
                    out[ends[n]] = code
                    ends[n] = ends[n] + jnp.minimum(code, 1)
            for n, out, _ in active:
                out[ends[n]] = 0
                ends[n] = ends[n] + (ends[n] & (PAIR - 1))
        return tuple(ends)

    first = tuple(jnp.int32(source * length) for length in lengths for source in range(2))
    ends = lax.fori_loop(0, rows, one_row, first)
    for k, out in enumerate(outs):
        pair = ends[2 * k], ends[2 * k + 1]
        most = jnp.maximum(pair[0], pair[1] - lengths[k])
        steps = lax.div(most + per_source - 1, per_source)
        steps_ref[k] = steps
        for source in range(2):
            def clear(at, carry, out=out):
                out[at] = 0
                return carry

            lax.fori_loop(pair[source], source * lengths[k] + steps * per_source, clear, 0)


def lists_of(codes, rows, slots, plan):
    lengths = [2 * capacity_of(rows, slots, len(c)) * PAIR for c in plan]
    smem = pl.BlockSpec(memory_space=pltpu.SMEM)
    *lists, steps = pl.pallas_call(
        functools.partial(lists_kernel, rows, slots, plan),
        out_shape=[jax.ShapeDtypeStruct((n,), jnp.int32) for n in lengths + [len(plan)]],
        in_specs=[smem],
        out_specs=[smem] * (len(plan) + 1),
        cost_estimate=SMALL,
        name="lists",
    )(codes)
    return lists, steps


def capacity_of(rows, slots, parts):
    tasks = (rows * slots + rows * parts * (PAIR - 1)) // PAIR
    return (-(-tasks // LANES) + 1) * LANES


def add_listed(codes_ref, steps, a_refs, v_all, blocks, sems, total):
    block = blocks.shape[-1]
    per_source = LANES * PAIR
    length = codes_ref.shape[0] // len(a_refs)

    def fetch(step):
        slot = lax.rem(step, DEPTH)
        for s, a_ref in enumerate(a_refs):
            for n in range(per_source):
                code = codes_ref[s * length + step * per_source + n]
                block_id = (code >> V_BITS) & ((1 << BLOCK_BITS) - 1)
                pltpu.make_async_copy(
                    a_ref.at[block_id], blocks.at[slot, s * per_source + n], sems.at[slot]
                ).start()

    for ahead in range(DEPTH - 1):
        @pl.when(ahead < steps)
        def _():
            fetch(ahead)

    def run():
        def one(step, carry):
            slot = lax.rem(step, DEPTH)

            @pl.when(step + DEPTH - 1 < steps)
            def _():
                fetch(step + DEPTH - 1)

            pltpu.make_async_copy(blocks.at[slot], blocks.at[slot], sems.at[slot]).wait()
            products = []
            for s in range(len(a_refs)):
                for n in range(LANES):
                    left, right = [], []
                    for g in range(PAIR):
                        at = n * PAIR + g
                        code = codes_ref[s * length + step * per_source + at]
                        if g == 0:
                            row = code >> (BLOCK_BITS + V_BITS)
                        start = pl.multiple_of((code & ((1 << V_BITS) - 1)) * block, block)
                        left.append(blocks[slot, s * per_source + at])
                        right.append(v_all[pl.ds(start, block), :])
                    product = jnp.dot(
                        jnp.concatenate(left, axis=1),
                        jnp.concatenate(right, axis=0),
                        preferred_element_type=jnp.float32,
                    )
                    products.append((row, product))
            for row, product in products:
                total[row] += product
            return carry

        lax.fori_loop(0, steps, one, 0)

    return run


def list_scratch(v_pieces, block):
    v_rows = block + sum(v.shape[0] for v in v_pieces)
    return [
        pltpu.VMEM((v_rows, block), jnp.bfloat16),
        pltpu.VMEM((DEPTH, 2 * LANES * PAIR, block, block), jnp.bfloat16),
        pltpu.SemaphoreType.DMA((DEPTH,)),
    ]


def copies_of(pairs, sems):
    copies = [pltpu.make_async_copy(a, b, sems.at[n]) for n, (a, b) in enumerate(pairs)]
    for copy in copies:
        copy.start()
    return copies


def v_places(v_refs, v_all, block):
    places, at = [], block
    for ref in v_refs:
        places.append((ref, v_all.at[pl.ds(at, ref.shape[0])]))
        at += ref.shape[0]
    return places


def later_kernel(pieces, codes_ref, steps_ref, me_ref, own_ref, other_ref, *refs):
    images, v_refs, refs = refs[:2], refs[2 : 2 + pieces], refs[2 + pieces :]
    out_ref, v_all, blocks, a_sems, sems = refs
    block = out_ref.shape[1]
    pairs = v_places(v_refs, v_all, block)
    for n, ref in enumerate(images):
        pairs.append((ref.at[1], out_ref.at[pl.ds(me_ref[1 + n], ref.shape[1])]))
    copies = copies_of(pairs, sems)
    run = add_listed(
        codes_ref, steps_ref[0], (own_ref, other_ref), v_all, blocks, a_sems, out_ref
    )
    v_all[pl.ds(0, block), :] = jnp.zeros((block, block), v_all.dtype)
    for copy in copies:
        copy.wait()
    run()


def later_image(codes, steps, me, own, other, images, v_pieces):
    block = own.shape[-1]
    shape = (sum(image.shape[1] for image in images), block, block)
    return pl.pallas_call(
        functools.partial(later_kernel, len(v_pieces)),
        out_shape=jax.ShapeDtypeStruct(shape, jnp.float32),
        grid_spec=pltpu.PrefetchScalarGridSpec(
            num_scalar_prefetch=3,
            grid=(1,),
            in_specs=anywhere(4 + len(v_pieces)),
            out_specs=pl.BlockSpec(shape, lambda i, *_: (0, 0, 0)),
            scratch_shapes=list_scratch(v_pieces, block)
            + [pltpu.SemaphoreType.DMA((len(v_pieces) + 2,))],
        ),
        compiler_params=pltpu.CompilerParams(vmem_limit_bytes=VMEM),
        cost_estimate=LARGE,
        name="later",
    )(codes, steps, me, own, other, *images, *v_pieces)


def last_kernel(pieces, codes_ref, steps_ref, me_ref, own_ref, other_ref, *refs):
    images, late_ref, refs = refs[:2], refs[2], refs[3:]
    v_refs, w_refs = refs[:pieces], refs[pieces : 4 + pieces]
    out_ref, v_all, blocks, a_sems, image, w_all, sems = refs[4 + pieces :]
    _, rows, block, _ = image.shape
    early = copies_of(v_places(v_refs, v_all, block) + [(late_ref, image.at[1])], sems)
    run = add_listed(
        codes_ref, steps_ref[1], (own_ref, other_ref), v_all, blocks, a_sems, image.at[1]
    )
    w_places = [(w_refs[q], w_all.at[q]) for q in range(4)]
    for n, ref in enumerate(images):
        w_places.append((ref.at[0], image.at[0, pl.ds(me_ref[1 + n], ref.shape[1])]))
    later = copies_of(w_places, sems.at[pl.ds(pieces + 1, 6)])
    v_all[pl.ds(0, block), :] = jnp.zeros((block, block), v_all.dtype)
    for copy in early:
        copy.wait()
    run()
    for copy in later:
        copy.wait()
    length = rows // 4
    total = None
    for q in range(4):
        terms = []
        for part in range(2):
            here = image[part, pl.ds((me_ref[0] ^ q) * length, length)]
            here = here.reshape(length * block, block)
            upper = here.astype(jnp.bfloat16)
            terms += [upper, (here - upper.astype(jnp.float32)).astype(jnp.bfloat16)]
        term = jnp.dot(
            w_all[q], jnp.concatenate(terms, axis=1), preferred_element_type=jnp.float32
        )
        total = term if total is None else total + term
    mine = me_ref[0] >> 1
    count, _, tile, _ = out_ref.shape
    for part, place in ((0, mine), (1, 1 - mine)):
        first = 2 * part * block
        both = total[:, first : first + block] + total[:, first + block : first + 2 * block]
        out_ref[:, place] = both.reshape(count, tile, block)


def last_projected(codes, steps, me, own, other, images, late, v_pieces, w_pieces, devices):
    rows, block, _ = late.shape
    basis, length = w_pieces[0].shape
    shape = (devices, 2, basis // devices, block)
    return pl.pallas_call(
        functools.partial(last_kernel, len(v_pieces)),
        out_shape=jax.ShapeDtypeStruct(shape, jnp.float32),
        grid_spec=pltpu.PrefetchScalarGridSpec(
            num_scalar_prefetch=3,
            grid=(1,),
            in_specs=anywhere(9 + len(v_pieces)),
            out_specs=pl.BlockSpec(shape, lambda i, *_: (0, 0, 0, 0)),
            scratch_shapes=list_scratch(v_pieces, block)
            + [
                pltpu.VMEM((2, rows, block, block), jnp.float32),
                pltpu.VMEM((4, basis, length), jnp.bfloat16),
                pltpu.SemaphoreType.DMA((len(v_pieces) + 7,)),
            ],
        ),
        compiler_params=pltpu.CompilerParams(vmem_limit_bytes=VMEM),
        cost_estimate=SMALL,
        name="last_projected",
    )(codes, steps, me, own, other, *images, late, *v_pieces, *w_pieces)


def shards(basis_v, basis_w, couplings, coupling_cols):
    rows, slots, block = couplings.shape[:3]
    regions, columns = lax.axis_size("region"), lax.axis_size("col")
    assert columns == 4 and regions % 2 == 0 and rows * slots <= 1 << BLOCK_BITS
    region, col = lax.axis_index("region"), lax.axis_index("col")
    odd = region % 2
    half = rows // 2

    own_a = cut(basis_v, odd * half, half * block, block)
    near_a, side_a = to_near(own_a), to_side(own_a)
    here = after(coupling_cols, own_a) - (region * rows - rows)
    there = to_core(here)
    other = to_core(after(couplings, there))
    own_b = cut(after(basis_v, there), (1 - odd) * half, half * block, block)
    near_b, side_b = to_near(own_b), to_side(own_b)
    w_own = basis_w.T

    cols = jnp.concatenate([here, there], axis=1)
    near_base = jnp.where(odd == 1, 0, 2 * rows)
    far_base = 2 * rows - near_base
    first, second = (1 - odd) * half, odd * half
    near_at = [near_base + first, near_base + second]
    far_at = [far_base + first, far_base + second]
    own_at = [rows + second, rows + first]
    me = jnp.stack([col, first, second]).astype(jnp.int32)

    both = jnp.stack([here, there])[None]
    in_near = both // rows == near_base // rows
    in_far = both // rows == far_base // rows
    is_a = (both % rows >= half) == (odd == 0)
    kind = jnp.arange(2, dtype=jnp.int32)[:, None, None, None]
    row = jnp.arange(rows, dtype=jnp.int32)[:, None]
    summed_early = (row >= half) == (odd == 0)
    taken = jnp.where(
        kind == 0, (in_near & (~is_a | summed_early)) | (in_far & is_a), in_far & ~is_a
    )
    piece = jnp.where(kind == 0, jnp.where(in_far, 2, jnp.where(is_a, 0, 1)), 0)
    block_id = row * slots + jnp.arange(slots, dtype=jnp.int32)[None, :]
    codes = (row << (BLOCK_BITS + V_BITS)) + (block_id << V_BITS)
    codes = jnp.where(taken, codes + 1 + piece * half + both % half, 0).reshape(-1)
    (later, last), steps = lists_of(codes, rows, slots, ((0,), (1,)))

    near_a, steps, cols, me, w_own = together(near_a, steps, cols, me, w_own)
    far_a, near_side_a = onward(near_a), to_near(side_a)

    near_b, side_b, other = together(near_b, side_b, other)
    far_b, passing = onward(near_b), beyond(side_b)
    w_side = to_side(after(w_own, near_b))
    pieces = [basis_v, near_a, near_b, far_a, side_a, side_b]
    at = [jnp.int32(rows), *near_at, far_at[0], *own_at]
    fills = [(far_at[1], half, 0), (near_base, rows, 1), (far_base, rows, 1)]
    early = image_of(
        cols, couplings, other, pieces, at, (0, 0, 0, 0, 1, 1), fills, first, half
    )

    early, near_side_a, passing = together(early, near_side_a, passing)
    far_side_b = to_near(passing)
    far_side_a, near_side_b = onward(near_side_a), to_near(after(side_b, passing))
    pieces = [basis_v, near_a, near_b, far_a, far_b, side_a, side_b, near_side_a]
    at = [jnp.int32(rows), *near_at, *far_at, *own_at, near_at[0]]
    fills = [(near_at[1], half, 1), (far_base, rows, 1)]
    rest = image_of(
        cols, couplings, other, pieces, at, (0, 0, 0, 0, 0, 1, 1, 1), fills, second, half
    )
    images = [early, rest]
    rest, w_own, w_side = together(rest, w_own, w_side)
    w_pieces = [w_own, to_core(w_own), w_side, to_core(w_side)]
    images = [early, rest]
    own_list = couplings.reshape(rows * slots, block, block)
    other_list = other.reshape(rows * slots, block, block)
    pieces = [near_side_a, near_side_b, far_side_a]
    image = later_image(later, steps, me, own_list, other_list, images, pieces)

    sent = last_projected(
        last, steps, me, own_list, other_list, images, image, [far_side_b], w_pieces,
        regions * columns,
    )
    received = lax.all_to_all(sent, EVERY, 0, 0, tiled=True)
    tile = sent.shape[2]
    summed = received.reshape(regions, columns // 2, 2, 2, tile, block).sum(axis=(0, 1))
    return summed.transpose(2, 1, 0, 3).reshape(tile, columns * block)


def solution(mesh):
    in_specs = (
        P("region", "col"),
        P(("region", "col"), None),
        P("region", "col", None, None),
        P("region", "col"),
    )
    out_specs = P(("region", "col"), None)
    return jax.shard_map(shards, mesh=mesh, in_specs=in_specs, out_specs=out_specs, check_vma=False)
```

```python
import functools

import jax
import jax.numpy as jnp
from jax import lax
from jax.experimental import pallas as pl
from jax.experimental.pallas import tpu as pltpu
from jax.sharding import PartitionSpec as P

EVERY = ("region", "col")
VMEM = 34 * 2**20
PAIR = 2
LANES = 8
DEPTH = 5
V_BITS, BLOCK_BITS = 8, 10
SMALL = pl.CostEstimate(flops=1, bytes_accessed=1, transcendentals=0)
LARGE = pl.CostEstimate(flops=10**12, bytes_accessed=10**9, transcendentals=0)


def moved(array, axis, target):
    count = lax.axis_size(axis)
    pairs = [(i, target(i)) for i in range(count)]
    return lax.ppermute(array, axis, [(i, j) for i, j in pairs if 0 <= j < count])


def to_core(array):
    return moved(array, "col", lambda c: c ^ 1)


def to_side(array):
    return moved(array, "col", lambda c: c ^ 2)


def to_near(array):
    return moved(array, "region", lambda r: r ^ 1)


def beyond(array):
    return moved(array, "region", lambda r: r + 2 if r % 2 else r - 2)


def onward(array):
    return moved(array, "region", lambda r: r - 2 if r % 2 else r + 2)


def together(*arrays):
    return lax.optimization_barrier(arrays)


def after(array, *others):
    return together(array, *others)[0]


def largest_divisor(length, limit):
    return max(d for d in range(1, limit + 1) if length % d == 0)


def anywhere(count):
    return [pl.BlockSpec(memory_space=pl.ANY)] * count


def image_kernel(group, parts, fills, cols_ref, offs_ref, own_ref, other_ref, *refs):
    pieces = len(parts)
    v_refs, refs = refs[:pieces], refs[pieces:]
    out_ref, v_all, blocks, sums, v_sems, a_sems, out_sems = refs
    depth, _, _, slots, block, _ = blocks.shape
    count = out_ref.shape[1]
    groups = count // group
    first = offs_ref[pieces + len(fills)]

    def place(n, rows, part):
        start = pl.multiple_of(offs_ref[n] * block, block)
        return pl.ds(start, rows), pl.ds(part * block, block)

    def read(g):
        slot = lax.rem(g, depth)
        here = pl.ds(first + g * group, group)
        return [
            pltpu.make_async_copy(ref.at[here], blocks.at[slot, n], a_sems.at[slot, n])
            for n, ref in enumerate((own_ref, other_ref))
        ]

    def write(g):
        slot = lax.rem(g, 2)
        return pltpu.make_async_copy(
            sums.at[slot], out_ref.at[:, pl.ds(g * group, group)], out_sems.at[slot]
        )

    copies = []
    for p, ref in enumerate(v_refs):
        rows = ref.shape[0]
        target = v_all.at[place(p, rows, parts[p])]
        copies.append(pltpu.make_async_copy(ref, target, v_sems.at[p]))
    for copy in copies:
        copy.start()
    for g in range(depth - 1):
        for copy in read(g):
            copy.start()
    for n, (rows, part) in enumerate(fills):
        at = place(pieces + n, rows, part)
        v_all[at] = jnp.zeros((rows, block), v_all.dtype)
    for copy in copies:
        copy.wait()

    def one(g, carry):
        slot, out_slot = lax.rem(g, depth), lax.rem(g, 2)

        @pl.when(g + depth - 1 < groups)
        def _():
            for copy in read(g + depth - 1):
                copy.start()

        for copy in read(g):
            copy.wait()

        @pl.when(g >= 2)
        def _():
            write(g - 2).wait()

        for r in range(group):
            left, right = [], []
            for n in range(2):
                for s in range(slots):
                    code = cols_ref[first + g * group + r, n * slots + s]
                    left.append(blocks[slot, n, r, s])
                    right.append(v_all[pl.ds(pl.multiple_of(code * block, block), block), :])
            product = jnp.dot(
                jnp.concatenate(left, axis=1),
                jnp.concatenate(right, axis=0),
                preferred_element_type=jnp.float32,
            )
            for part in range(2):
                sums[out_slot, part, r] = product[:, part * block : (part + 1) * block]
        write(g).start()
        return carry

    lax.fori_loop(0, groups, one, 0)
    for g in range(max(groups - 2, 0), groups):
        write(g).wait()


def image_of(cols, own, other, v_pieces, places, parts, fills, start, count):
    rows, slots, block = own.shape[:3]
    group = largest_divisor(count, 4)
    depth = min(3, count // group + 1)
    pieces = len(v_pieces)
    offs = jnp.stack([*places, *[f[0] for f in fills], start]).astype(jnp.int32)
    fill_shapes = tuple((f[1] * block, f[2]) for f in fills)
    return pl.pallas_call(
        functools.partial(image_kernel, group, parts, fill_shapes),
        out_shape=jax.ShapeDtypeStruct((2, count, block, block), jnp.float32),
        grid_spec=pltpu.PrefetchScalarGridSpec(
            num_scalar_prefetch=2,
            grid=(1,),
            in_specs=anywhere(2 + pieces),
            out_specs=pl.BlockSpec(memory_space=pl.ANY),
            scratch_shapes=[
                pltpu.VMEM((3 * rows * block, 2 * block), jnp.bfloat16),
                pltpu.VMEM((depth, 2, group, slots, block, block), jnp.bfloat16),
                pltpu.VMEM((2, 2, group, block, block), jnp.float32),
                pltpu.SemaphoreType.DMA((pieces,)),
                pltpu.SemaphoreType.DMA((depth, 2)),
                pltpu.SemaphoreType.DMA((2,)),
            ],
        ),
        compiler_params=pltpu.CompilerParams(vmem_limit_bytes=VMEM),
        cost_estimate=SMALL,
        name="image",
    )(cols, offs, own, other, *v_pieces)


def cut_kernel(block, start_ref, v_ref, out_ref, stage, sems):
    start = pl.multiple_of(start_ref[0] * block, block)
    read = pltpu.make_async_copy(v_ref.at[pl.ds(start, stage.shape[0])], stage, sems.at[0])
    write = pltpu.make_async_copy(stage, out_ref, sems.at[1])
    read.start()
    read.wait()
    write.start()
    write.wait()


def cut(array, start, length, block):
    part = jax.ShapeDtypeStruct((length, array.shape[1]), array.dtype)
    return pl.pallas_call(
        functools.partial(cut_kernel, block),
        out_shape=part,
        grid_spec=pltpu.PrefetchScalarGridSpec(
            num_scalar_prefetch=1,
            grid=(1,),
            in_specs=anywhere(1),
            out_specs=pl.BlockSpec(memory_space=pl.ANY),
            scratch_shapes=[pltpu.VMEM(part.shape, part.dtype), pltpu.SemaphoreType.DMA((2,))],
        ),
        cost_estimate=SMALL,
        name="cut",
    )(jnp.reshape(start, (1,)).astype(jnp.int32), array)


def lists_kernel(rows, slots, plan, codes_ref, *refs):
    outs, steps_ref = refs[:-1], refs[-1]
    per_source = LANES * PAIR
    size = 2 * rows * slots
    lengths = [out.shape[0] // 2 for out in outs]
    turns = max(len(classes) for classes in plan)

    def one_row(row, ends):
        ends = list(ends)
        for turn in range(turns):
            active = [
                (2 * k + source, out, classes[turn] * size + (source * rows + row) * slots)
                for k, (out, classes) in enumerate(zip(outs, plan))
                if turn < len(classes)
                for source in range(2)
            ]
            for s in range(slots):
                for n, out, base in active:
                    code = codes_ref[base + s]
                    out[ends[n]] = code
                    ends[n] = ends[n] + jnp.minimum(code, 1)
            for n, out, _ in active:
                out[ends[n]] = 0
                ends[n] = ends[n] + (ends[n] & (PAIR - 1))
        return tuple(ends)

    first = tuple(jnp.int32(source * length) for length in lengths for source in range(2))
    ends = lax.fori_loop(0, rows, one_row, first)
    for k, out in enumerate(outs):
        pair = ends[2 * k], ends[2 * k + 1]
        most = jnp.maximum(pair[0], pair[1] - lengths[k])
        steps = lax.div(most + per_source - 1, per_source)
        steps_ref[k] = steps
        for source in range(2):
            def clear(at, carry, out=out):
                out[at] = 0
                return carry

            lax.fori_loop(pair[source], source * lengths[k] + steps * per_source, clear, 0)


def lists_of(codes, rows, slots, plan):
    lengths = [2 * capacity_of(rows, slots, len(c)) * PAIR for c in plan]
    smem = pl.BlockSpec(memory_space=pltpu.SMEM)
    *lists, steps = pl.pallas_call(
        functools.partial(lists_kernel, rows, slots, plan),
        out_shape=[jax.ShapeDtypeStruct((n,), jnp.int32) for n in lengths + [len(plan)]],
        in_specs=[smem],
        out_specs=[smem] * (len(plan) + 1),
        cost_estimate=SMALL,
        name="lists",
    )(codes)
    return lists, steps


def capacity_of(rows, slots, parts):
    tasks = (rows * slots + rows * parts * (PAIR - 1)) // PAIR
    return (-(-tasks // LANES) + 1) * LANES


def add_listed(codes_ref, steps, a_refs, v_all, blocks, sems, total):
    block = blocks.shape[-1]
    per_source = LANES * PAIR
    length = codes_ref.shape[0] // len(a_refs)

    def fetch(step):
        slot = lax.rem(step, DEPTH)
        for s, a_ref in enumerate(a_refs):
            for n in range(per_source):
                code = codes_ref[s * length + step * per_source + n]
                block_id = (code >> V_BITS) & ((1 << BLOCK_BITS) - 1)
                pltpu.make_async_copy(
                    a_ref.at[block_id], blocks.at[slot, s * per_source + n], sems.at[slot]
                ).start(priority=s)

    for ahead in range(DEPTH - 1):
        @pl.when(ahead < steps)
        def _():
            fetch(ahead)

    def run():
        def one(step, carry):
            slot = lax.rem(step, DEPTH)

            @pl.when(step + DEPTH - 1 < steps)
            def _():
                fetch(step + DEPTH - 1)

            pltpu.make_async_copy(blocks.at[slot], blocks.at[slot], sems.at[slot]).wait()
            products = []
            for s in range(len(a_refs)):
                for n in range(LANES):
                    left, right = [], []
                    for g in range(PAIR):
                        at = n * PAIR + g
                        code = codes_ref[s * length + step * per_source + at]
                        if g == 0:
                            row = code >> (BLOCK_BITS + V_BITS)
                        start = pl.multiple_of((code & ((1 << V_BITS) - 1)) * block, block)
                        left.append(blocks[slot, s * per_source + at])
                        right.append(v_all[pl.ds(start, block), :])
                    product = jnp.dot(
                        jnp.concatenate(left, axis=1),
                        jnp.concatenate(right, axis=0),
                        preferred_element_type=jnp.float32,
                    )
                    products.append((row, product))
            for row, product in products:
                total[row] += product
            return carry

        lax.fori_loop(0, steps, one, 0)

    return run


def list_scratch(v_pieces, block):
    v_rows = block + sum(v.shape[0] for v in v_pieces)
    return [
        pltpu.VMEM((v_rows, block), jnp.bfloat16),
        pltpu.VMEM((DEPTH, 2 * LANES * PAIR, block, block), jnp.bfloat16),
        pltpu.SemaphoreType.DMA((DEPTH,)),
    ]


def copies_of(pairs, sems):
    copies = [pltpu.make_async_copy(a, b, sems.at[n]) for n, (a, b) in enumerate(pairs)]
    for copy in copies:
        copy.start()
    return copies


def v_places(v_refs, v_all, block):
    places, at = [], block
    for ref in v_refs:
        places.append((ref, v_all.at[pl.ds(at, ref.shape[0])]))
        at += ref.shape[0]
    return places


def later_kernel(pieces, codes_ref, steps_ref, me_ref, own_ref, other_ref, *refs):
    images, v_refs, refs = refs[:2], refs[2 : 2 + pieces], refs[2 + pieces :]
    out_ref, v_all, blocks, a_sems, sems = refs
    block = out_ref.shape[1]
    pairs = v_places(v_refs, v_all, block)
    for n, ref in enumerate(images):
        pairs.append((ref.at[1], out_ref.at[pl.ds(me_ref[1 + n], ref.shape[1])]))
    copies = copies_of(pairs, sems)
    run = add_listed(
        codes_ref, steps_ref[0], (own_ref, other_ref), v_all, blocks, a_sems, out_ref
    )
    v_all[pl.ds(0, block), :] = jnp.zeros((block, block), v_all.dtype)
    for copy in copies:
        copy.wait()
    run()


def later_image(codes, steps, me, own, other, images, v_pieces):
    block = own.shape[-1]
    shape = (sum(image.shape[1] for image in images), block, block)
    return pl.pallas_call(
        functools.partial(later_kernel, len(v_pieces)),
        out_shape=jax.ShapeDtypeStruct(shape, jnp.float32),
        grid_spec=pltpu.PrefetchScalarGridSpec(
            num_scalar_prefetch=3,
            grid=(1,),
            in_specs=anywhere(4 + len(v_pieces)),
            out_specs=pl.BlockSpec(shape, lambda i, *_: (0, 0, 0)),
            scratch_shapes=list_scratch(v_pieces, block)
            + [pltpu.SemaphoreType.DMA((len(v_pieces) + 2,))],
        ),
        compiler_params=pltpu.CompilerParams(vmem_limit_bytes=VMEM),
        cost_estimate=LARGE,
        name="later",
    )(codes, steps, me, own, other, *images, *v_pieces)


def last_kernel(pieces, codes_ref, steps_ref, me_ref, own_ref, other_ref, *refs):
    images, late_ref, refs = refs[:2], refs[2], refs[3:]
    v_refs, w_refs = refs[:pieces], refs[pieces : 4 + pieces]
    out_ref, v_all, blocks, a_sems, image, w_all, sems = refs[4 + pieces :]
    _, rows, block, _ = image.shape
    early = copies_of(v_places(v_refs, v_all, block) + [(late_ref, image.at[1])], sems)
    run = add_listed(
        codes_ref, steps_ref[1], (own_ref, other_ref), v_all, blocks, a_sems, image.at[1]
    )
    w_places = [(w_refs[q], w_all.at[q]) for q in range(4)]
    for n, ref in enumerate(images):
        w_places.append((ref.at[0], image.at[0, pl.ds(me_ref[1 + n], ref.shape[1])]))
    later = copies_of(w_places, sems.at[pl.ds(pieces + 1, 6)])
    v_all[pl.ds(0, block), :] = jnp.zeros((block, block), v_all.dtype)
    for copy in early:
        copy.wait()
    run()
    for copy in later:
        copy.wait()
    length = rows // 4
    total = None
    for q in range(4):
        terms = []
        for part in range(2):
            here = image[part, pl.ds((me_ref[0] ^ q) * length, length)]
            here = here.reshape(length * block, block)
            upper = here.astype(jnp.bfloat16)
            terms += [upper, (here - upper.astype(jnp.float32)).astype(jnp.bfloat16)]
        term = jnp.dot(
            w_all[q], jnp.concatenate(terms, axis=1), preferred_element_type=jnp.float32
        )
        total = term if total is None else total + term
    mine = me_ref[0] >> 1
    count, _, tile, _ = out_ref.shape
    for part, place in ((0, mine), (1, 1 - mine)):
        first = 2 * part * block
        both = total[:, first : first + block] + total[:, first + block : first + 2 * block]
        out_ref[:, place] = both.reshape(count, tile, block)


def last_projected(codes, steps, me, own, other, images, late, v_pieces, w_pieces, devices):
    rows, block, _ = late.shape
    basis, length = w_pieces[0].shape
    shape = (devices, 2, basis // devices, block)
    return pl.pallas_call(
        functools.partial(last_kernel, len(v_pieces)),
        out_shape=jax.ShapeDtypeStruct(shape, jnp.float32),
        grid_spec=pltpu.PrefetchScalarGridSpec(
            num_scalar_prefetch=3,
            grid=(1,),
            in_specs=anywhere(9 + len(v_pieces)),
            out_specs=pl.BlockSpec(shape, lambda i, *_: (0, 0, 0, 0)),
            scratch_shapes=list_scratch(v_pieces, block)
            + [
                pltpu.VMEM((2, rows, block, block), jnp.float32),
                pltpu.VMEM((4, basis, length), jnp.bfloat16),
                pltpu.SemaphoreType.DMA((len(v_pieces) + 7,)),
            ],
        ),
        compiler_params=pltpu.CompilerParams(vmem_limit_bytes=VMEM),
        cost_estimate=SMALL,
        name="last_projected",
    )(codes, steps, me, own, other, *images, late, *v_pieces, *w_pieces)


def shards(basis_v, basis_w, couplings, coupling_cols):
    rows, slots, block = couplings.shape[:3]
    regions, columns = lax.axis_size("region"), lax.axis_size("col")
    assert columns == 4 and regions % 2 == 0 and rows * slots <= 1 << BLOCK_BITS
    region, col = lax.axis_index("region"), lax.axis_index("col")
    odd = region % 2
    half = rows // 2

    own_a = cut(basis_v, odd * half, half * block, block)
    near_a, side_a = to_near(own_a), to_side(own_a)
    here = after(coupling_cols, own_a) - (region * rows - rows)
    there = to_core(here)
    other = to_core(after(couplings, there))
    own_b = cut(after(basis_v, there), (1 - odd) * half, half * block, block)
    near_b, side_b = to_near(own_b), to_side(own_b)
    w_own = basis_w.T

    cols = jnp.concatenate([here, there], axis=1)
    near_base = jnp.where(odd == 1, 0, 2 * rows)
    far_base = 2 * rows - near_base
    first, second = (1 - odd) * half, odd * half
    near_at = [near_base + first, near_base + second]
    far_at = [far_base + first, far_base + second]
    own_at = [rows + second, rows + first]
    me = jnp.stack([col, first, second]).astype(jnp.int32)

    both = jnp.stack([here, there])[None]
    in_near = both // rows == near_base // rows
    in_far = both // rows == far_base // rows
    is_a = (both % rows >= half) == (odd == 0)
    kind = jnp.arange(2, dtype=jnp.int32)[:, None, None, None]
    row = jnp.arange(rows, dtype=jnp.int32)[:, None]
    summed_early = (row >= half) == (odd == 0)
    taken = jnp.where(
        kind == 0, (in_near & (~is_a | summed_early)) | (in_far & is_a), in_far & ~is_a
    )
    piece = jnp.where(kind == 0, jnp.where(in_far, 2, jnp.where(is_a, 0, 1)), 0)
    block_id = row * slots + jnp.arange(slots, dtype=jnp.int32)[None, :]
    codes = (row << (BLOCK_BITS + V_BITS)) + (block_id << V_BITS)
    codes = jnp.where(taken, codes + 1 + piece * half + both % half, 0).reshape(-1)
    (later, last), steps = lists_of(codes, rows, slots, ((0,), (1,)))

    near_a, steps, cols, me, w_own = together(near_a, steps, cols, me, w_own)
    far_a, near_side_a = onward(near_a), to_near(side_a)

    near_b, side_b, other = together(near_b, side_b, other)
    far_b, passing = onward(near_b), beyond(side_b)
    w_side = to_side(after(w_own, near_b))
    pieces = [basis_v, near_a, near_b, far_a, side_a, side_b]
    at = [jnp.int32(rows), *near_at, far_at[0], *own_at]
    fills = [(far_at[1], half, 0), (near_base, rows, 1), (far_base, rows, 1)]
    early = image_of(
        cols, couplings, other, pieces, at, (0, 0, 0, 0, 1, 1), fills, first, half
    )

    early, near_side_a, passing = together(early, near_side_a, passing)
    far_side_b = to_near(passing)
    far_side_a, near_side_b = onward(near_side_a), to_near(after(side_b, passing))
    pieces = [basis_v, near_a, near_b, far_a, far_b, side_a, side_b, near_side_a]
    at = [jnp.int32(rows), *near_at, *far_at, *own_at, near_at[0]]
    fills = [(near_at[1], half, 1), (far_base, rows, 1)]
    rest = image_of(
        cols, couplings, other, pieces, at, (0, 0, 0, 0, 0, 1, 1, 1), fills, second, half
    )
    images = [early, rest]
    rest, w_own, w_side = together(rest, w_own, w_side)
    w_pieces = [w_own, to_core(w_own), w_side, to_core(w_side)]
    images = [early, rest]
    own_list = couplings.reshape(rows * slots, block, block)
    other_list = other.reshape(rows * slots, block, block)
    pieces = [near_side_a, near_side_b, far_side_a]
    image = later_image(later, steps, me, own_list, other_list, images, pieces)

    sent = last_projected(
        last, steps, me, own_list, other_list, images, image, [far_side_b], w_pieces,
        regions * columns,
    )
    received = lax.all_to_all(sent, EVERY, 0, 0, tiled=True)
    tile = sent.shape[2]
    summed = received.reshape(regions, columns // 2, 2, 2, tile, block).sum(axis=(0, 1))
    return summed.transpose(2, 1, 0, 3).reshape(tile, columns * block)


def solution(mesh):
    in_specs = (
        P("region", "col"),
        P(("region", "col"), None),
        P("region", "col", None, None),
        P("region", "col"),
    )
    out_specs = P(("region", "col"), None)
    return jax.shard_map(shards, mesh=mesh, in_specs=in_specs, out_specs=out_specs, check_vma=False)
```
